32 devices in a mesh: dp: 2 (over x), pipe: 4 (over y, core), tensor: 4 (over z).
Axes of the slice: x: 2, y: 2, z: 4, core: 2. Of those that a mesh axis runs over, the one named last changes fastest.
Arguments:
- grad_out: bfloat16 [8, 128, 4096], P(None, 'dp', 'tensor'), may hold values from -6 to 6
- activations: bfloat16 [4, 3, 8, 128, 4096], P('pipe', None, None, 'dp', 'tensor'), may hold values from -6 to 6
- mixing: bfloat16 [4, 3, 32, 128, 128], P('pipe', None, 'tensor'), may hold values from -0.1875 to 0.1875
- proj_tiles: bfloat16 [4, 3, 8, 128, 128], P('pipe'), may hold values from -0.1875 to 0.1875
- proj_blocks: int32 [4, 3, 8], P('pipe'), may hold values from 0 to 31, all different within a row
- section_sizes: int32 [4], replicated, may hold values from 1 to 3, 8 in all
Outputs:
- segment_grads: bfloat16 [4, 8, 128, 4096], P('pipe', None, 'dp', 'tensor')
- sketches: float32 [4, 3, 8, 4096], P('pipe')
The draws below stay inside these ranges and needn't reach their ends.
Inputs may be any that keep to these rules, and one draw needn't show every extreme that they name: `section_sizes`: each segment holds 1 to 3 layers, 8 in all, some segment exactly 3. `proj_blocks`: the 8 blocks of one slot are distinct.
All inputs are finite; a program needn't handle non-finite values.
Results may differ from the reference program's by a relative error of at most 0.0074.
Values may be sent and summed in bfloat16 or wider, within the bound.
No kernel may reach another device: no remote copies, remote signals or barrier semaphores. Data moves between devices by JAX's collectives and lax.ppermute only.
A program may use at most 64 MiB of HBM per device.

```python
import math
import jax
import jax.numpy as jnp
import numpy as np
from jax import lax

D = 4096
HS = 128
RANK = 64
NP = 8
SLOTS = 3
MB = 8
HEADS = 32
MB_TOK = 128
LAYERS = 8
N_PIPE = 4


def block_scale(own_key, dims, pieces, smallest, top_value):
    level = 1.0
    for position, shards_of in pieces:
        heights = jax.random.uniform(jax.random.fold_in(jax.random.fold_in(own_key, 6), position), (shards_of,), jnp.float32, smallest / len(pieces), top_value / len(pieces))
        level = level * jnp.repeat(jnp.exp(heights), dims[position] // shards_of).reshape((-1,) + (1,) * (len(dims) - 1 - position))
    return level


def different_ones(rng, rows, number_of, top, lift):
    order = jax.random.permutation(jax.random.fold_in(rng, 1), number_of)
    pull = order
    for power in range(3):
        pull = pull * pull // number_of
    pull = pull * lift // number_of
    chance = jax.random.randint(jax.random.fold_in(rng, 2), (rows, number_of), 0, 4096) + pull
    sure = jax.random.permutation(jax.random.fold_in(rng, 3), rows)[jnp.arange(number_of) % rows]
    chance = jnp.where(jnp.arange(rows)[:, None] == sure[None, :], 1 << 14, chance)
    priority = chance * number_of + jnp.arange(number_of)
    return lax.top_k(priority.astype(jnp.int32), top)[1].astype(jnp.int32)


def profile(count, total, limit, skew):
    portions = [(1 << 20) // math.isqrt(rank ** skew) + 1 for rank in range(2, count + 1)]
    rest, given = total - limit - (count - 1), [1] * (count - 1)
    while rest > 0:
        free = [i for i in range(count - 1) if given[i] < limit]
        pool, left = sum([portions[i] for i in free]), rest
        for i in free:
            addition = min(limit - given[i], max(1, left * portions[i] // pool), rest)
            given[i] = given[i] + addition
            rest = rest - addition
    return np.array([limit] + given)


def ragged_sizes(own_key, count, total, most, skew):
    if count == 2:
        one = jax.random.randint(own_key, (), max(1, total - most), min(most, total - 1) + 1)
        return jnp.stack([one, total - one])
    sizes = jnp.asarray(profile(count, total, most, skew), jnp.int32)
    twos = (count - 1) // 2
    donor, sink = sizes[1:1 + 2 * twos:2], sizes[2:2 + 2 * twos:2]
    margin = jnp.minimum(donor - 1, most - sink)
    passed = jax.random.randint(jax.random.fold_in(own_key, 1), (twos,), 0, 1 << 20) % (margin + 1)
    sizes = sizes.at[1:1 + 2 * twos:2].set(donor - passed).at[2:2 + 2 * twos:2].set(sink + passed)
    return sizes[jax.random.permutation(jax.random.fold_in(own_key, 2), count)]


def centred(rng, dims, width, bound, pieces=(), held_as=jnp.bfloat16):
    drawn = jax.random.normal(rng, dims, jnp.float32) * width
    if len(pieces) > 0:
        drawn = block_scale(rng, dims, pieces, -0.22, 0.18) * drawn
    return jnp.clip(drawn, min=-bound, max=bound).astype(held_as)


def setup_inputs(seed: int = 0) -> dict:
    seeds = jax.random.split(jax.random.key(seed), 7)
    return {
        "grad_out": centred(seeds[0], (MB, MB_TOK, D), 1.0, 6.0, ((1, 2), (2, 4))),
        "activations": centred(seeds[1], (N_PIPE, SLOTS, MB, MB_TOK, D), 1.0, 6.0, ((0, 4), (3, 2), (4, 4))),
        "mixing": centred(seeds[2], (N_PIPE, SLOTS, HEADS, HS, HS), (8 * HS) ** -0.5, 0.1875, ((0, 4), (2, 4))),
        "proj_tiles": centred(seeds[3], (N_PIPE, SLOTS, NP, HS, 2 * RANK), (NP * HS) ** -0.5, 0.1875, ((0, 4),)),
        "proj_blocks": different_ones(seeds[4], N_PIPE * SLOTS, D // HS, NP, 0).reshape((N_PIPE, SLOTS, NP)),
        "section_sizes": ragged_sizes(seeds[5], N_PIPE, LAYERS, SLOTS, 1).astype(jnp.int32),
    }


def silu_slope(value):
    sig = jax.nn.sigmoid(value)
    return sig * (1.0 + value * (1.0 - sig))

def reference(grad_out, activations, mixing, proj_tiles, proj_blocks, section_sizes):
    high = lax.Precision.HIGHEST
    scale = 1.0 / math.sqrt(MB_TOK)
    grad = grad_out
    segment_list = [None] * N_PIPE
    sketch_list = [None] * N_PIPE
    for segment in range(N_PIPE - 1, -1, -1):
        per_slot = [None] * SLOTS
        for slot in range(SLOTS - 1, -1, -1):
            live = slot < section_sizes[segment]
            heads_in = activations[segment, slot].reshape(MB, MB_TOK, HEADS, HS).astype(jnp.float32)
            weight = mixing[segment, slot].astype(jnp.float32)
            pre = jnp.einsum('mthc,hcd->mthd', heads_in, weight, precision=high)
            grad_heads = grad.reshape(MB, MB_TOK, HEADS, HS).astype(jnp.float32)
            delta = (grad_heads * silu_slope(pre)).astype(jnp.bfloat16)
            delta_wide = delta.astype(jnp.float32)
            back = jnp.einsum('mthd,hcd->mthc', delta_wide, weight, precision=high)
            moved = (grad_heads + back).reshape(MB, MB_TOK, D).astype(jnp.bfloat16)
            grad = jnp.where(live, moved, grad)
            blocks = proj_blocks[segment, slot].astype(jnp.int32)
            tiles = proj_tiles[segment, slot].astype(jnp.float32)
            picked_act = jnp.take(heads_in, blocks, axis=2)
            picked_delta = jnp.take(delta_wide, blocks, axis=2)
            act_proj = jnp.einsum('mtjc,jcr->mtr', picked_act, tiles[:, :, :RANK], precision=high)
            grad_proj = jnp.einsum('mtjc,jcr->mtr', picked_delta, tiles[:, :, RANK:], precision=high)
            sketch = jnp.einsum('mtr,mts->mrs', grad_proj, act_proj, precision=high) * scale
            per_slot[slot] = jnp.where(live, sketch.reshape(MB, RANK * RANK), jnp.zeros((MB, RANK * RANK), jnp.float32))
        segment_list[segment] = grad
        sketch_list[segment] = jnp.stack(per_slot)
    return (jnp.stack(segment_list), jnp.stack(sketch_list))
```

```python
import functools
import math

import jax
import jax.numpy as jnp
from jax import lax
from jax.experimental import pallas as pl
from jax.experimental.pallas import tpu as pltpu
from jax.sharding import PartitionSpec as P

F32 = jnp.float32
BF16 = jnp.bfloat16
VMEM = pl.BlockSpec(memory_space=pltpu.VMEM)
SMEM = pl.BlockSpec(memory_space=pltpu.SMEM)
PARAMS = pltpu.CompilerParams(vmem_limit_bytes=48 * 1024 * 1024)


def silu_slope(value):
    sig = 0.5 + 0.5 * jnp.tanh(0.5 * value)
    return sig * (1.0 + value * (1.0 - sig))


def left_lanes(shape, rank):
    return lax.broadcasted_iota(jnp.int32, shape, len(shape) - 1) < rank


def prep_kernel(place, blocks, tiles, acts, dense_g, act_sums, dense_a):
    slots, picks, head_size, both = tiles.shape
    rank = both // 2
    micro = acts.shape[1]
    heads = dense_g.shape[1] // head_size
    row = lax.broadcasted_iota(jnp.int32, (both, both), 0)
    col = lax.broadcasted_iota(jnp.int32, (both, both), 1)
    twice = (row == col % rank).astype(BF16)
    order = rank + jnp.where(col < rank // 2, 2 * col, 2 * col - rank + 1)
    split = jnp.logical_and(row == order, col < rank).astype(BF16)
    dense_a[...] = jnp.zeros_like(dense_a)
    dense_g[...] = jnp.zeros_like(dense_g)
    for k in range(slots):
        for j in range(picks):
            own = blocks[k, j] - place[0] * heads

            @pl.when(jnp.logical_and(own >= 0, own < heads))
            def _():
                rows = pl.ds(pl.multiple_of(own * head_size, head_size), head_size)
                tile = tiles[k, j]
                dense_a[k, rows, :] = jnp.dot(tile, twice, preferred_element_type=F32).astype(BF16)
                dense_g[k, rows, :] = jnp.dot(tile, split, preferred_element_type=F32).astype(BF16)

    half = micro // 2
    tokens = acts.shape[2]

    def project(k, _):
        first = acts[k, :half].reshape(half * tokens, -1)
        second = acts[k, half:].reshape(half * tokens, -1)
        one = jnp.dot(first, dense_a[k], preferred_element_type=F32)
        two = jnp.dot(second, dense_a[k], preferred_element_type=F32)
        act_sums[k] = jnp.where(left_lanes(one.shape, rank), one, two).astype(BF16)
        return 0

    lax.fori_loop(0, slots, project, 0)


def chain_kernel(step, place, *refs, sources, top):
    refs = list(refs)
    odd_in = refs.pop(0) if "odd" in sources else None
    even_in = refs.pop(0) if "even" in sources else None
    acts, mixing, grad, deltas = refs
    chunk, tokens, width = grad.shape
    heads, head_size = mixing.shape[1], mixing.shape[2]
    rows = chunk * tokens
    live, odd, active = place[1], place[2], place[3]
    at = (step - 1 + odd) * chunk

    def run():
        def slot(i, _):
            k = live - 1 - i
            for h in range(heads):
                lanes = slice(h * head_size, (h + 1) * head_size)
                act = acts[k, pl.ds(at, chunk), :, lanes].reshape(rows, head_size)
                weight = mixing[k, h]
                pre = jnp.dot(act, weight, preferred_element_type=F32)
                g = grad[:, :, lanes].reshape(rows, head_size).astype(F32)
                delta = (g * silu_slope(pre)).astype(BF16)
                back = lax.dot_general(delta, weight, (((1,), (1,)), ((), ())), preferred_element_type=F32)
                grad[:, :, lanes] = (g + back).astype(BF16).reshape(chunk, tokens, head_size)
                deltas[k, :, :, lanes] = delta.reshape(chunk, tokens, head_size)
            return 0

        lax.fori_loop(0, live, slot, 0)

    if odd_in is not None:

        @pl.when(jnp.logical_and(active == 1, odd == 1))
        def _():
            if top:
                grad[...] = odd_in[step * chunk : (step + 1) * chunk]
            else:
                grad[...] = odd_in[...]

    if even_in is not None:

        @pl.when(jnp.logical_and(active == 1, odd == 0))
        def _():
            grad[...] = even_in[...]

    if odd_in is None:
        wanted = jnp.logical_and(active == 1, odd == 0)
    elif even_in is None:
        wanted = jnp.logical_and(active == 1, odd == 1)
    else:
        wanted = active == 1

    pl.when(wanted)(run)


def sketch_kernel(place, *refs, count, pairs, scale):
    deltas = [refs[p * (count + 1) : (p + 1) * (count + 1)] for p in range(pairs)]
    dense_g, act_sums, out = refs[pairs * (count + 1) :]
    slots, chunk, tokens, width = deltas[0][0].shape
    both = dense_g.shape[2]
    rank = both // 2
    micro = out.shape[1]
    half = micro // 2
    live, odd, pair = place[1], place[2], place[4]

    def one(ref, c):
        for k in range(slots):

            @pl.when(k < live)
            def _():
                flat = ref[k].reshape(chunk * tokens, width)
                proj = jnp.dot(flat, dense_g[k], preferred_element_type=F32)
                for i in range(chunk):
                    m = c * chunk + i
                    rows = slice((m % half) * tokens, (m % half + 1) * tokens)
                    act = act_sums[k, rows, :]
                    other = pltpu.roll(act, rank, 1)
                    left = left_lanes(act.shape, rank)
                    act = jnp.where(left, act, other) if m < half else jnp.where(left, other, act)
                    full = lax.dot_general(
                        proj[i * tokens : (i + 1) * tokens],
                        act,
                        (((0,), (0,)), ((), ())),
                        precision=lax.Precision.HIGHEST,
                        preferred_element_type=F32,
                    )
                    even, uneven = full[: rank // 2], full[rank // 2 : rank]
                    res = jnp.where(left_lanes(even.shape, rank), even, uneven) * scale
                    out[k, m] = res.astype(BF16)

            @pl.when(k >= live)
            def _():
                out[k, c * chunk : (c + 1) * chunk] = jnp.zeros((chunk, rank // 2, both), BF16)

    for c in range(count):
        for p in range(pairs):
            for parity in (0, 1):

                @pl.when(jnp.logical_and(pair == p, odd == parity))
                def _():
                    one(deltas[p][c + 1 - parity], c)


def swap_sum(x, axis, by):
    peers = lax.axis_size(axis)
    other = lax.ppermute(x, axis, [(i, i ^ by) for i in range(peers)])
    return x.astype(F32) + other.astype(F32)


def all_sum(x, axes):
    x = x.astype(BF16)
    total = x.astype(F32)
    for axis in axes:
        peers = lax.axis_size(axis)
        if peers & (peers - 1):
            total = lax.psum(total, axis)
        else:
            by = 1
            while by < peers:
                total = swap_sum(total.astype(BF16), axis, by)
                by *= 2
    return total


def shards(grad_out, activations, mixing, proj_tiles, proj_blocks, section_sizes):
    sections = lax.axis_size("pipe")
    section = lax.axis_index("pipe")
    micro, tokens, width = grad_out.shape
    slots = activations.shape[1]
    head_size = mixing.shape[3]
    rank = proj_tiles.shape[4] // 2
    scale = 1.0 / math.sqrt(tokens * lax.axis_size("dp"))
    pairs = sections // 2
    count = 4
    chunk = micro // count
    acts, mix = activations[0], mixing[0]
    odd = section % 2
    pair = section // 2
    live = section_sizes[section]
    index = lax.axis_index("tensor")

    def place(p):
        here = (pair == pairs - 1 - p).astype(jnp.int32)
        return jnp.stack([index, live, odd, here, pairs - 1 - pair]).astype(jnp.int32)

    places = [place(p) for p in range(pairs)]
    dense_g, act_part = pl.pallas_call(
        prep_kernel,
        out_shape=(
            jax.ShapeDtypeStruct((slots, width, 2 * rank), BF16),
            jax.ShapeDtypeStruct((slots, micro // 2 * tokens, 2 * rank), BF16),
        ),
        in_specs=[SMEM, SMEM, VMEM, VMEM],
        out_specs=(VMEM, VMEM),
        scratch_shapes=[pltpu.VMEM((slots, width, 2 * rank), BF16)],
        compiler_params=PARAMS,
        name="prep",
    )(places[0], proj_blocks[0], proj_tiles[0], acts)
    act_sums = all_sum(act_part, ("tensor",))

    swap = [(i, i ^ 1) for i in range(sections)]
    from_above = [grad_out] * count
    all_deltas, all_grads = [], []
    for p in range(pairs):
        deltas, grads, below = [], [], []
        even_in = None
        for step in range(count + 1):
            odd_in = from_above[step] if step < count else None
            sources = [n for n, v in (("odd", odd_in), ("even", even_in)) if v is not None]
            ins = [v for v in (odd_in, even_in) if v is not None]
            grad, delta = pl.pallas_call(
                functools.partial(chain_kernel, step, sources=sources, top=p == 0),
                out_shape=(
                    jax.ShapeDtypeStruct((chunk, tokens, width), BF16),
                    jax.ShapeDtypeStruct((slots, chunk, tokens, width), BF16),
                ),
                in_specs=[SMEM] + [VMEM] * (len(ins) + 2),
                out_specs=(VMEM, VMEM),
                compiler_params=PARAMS,
                name="chain",
            )(places[p], *ins, acts, mix)
            if step < count:
                even_in = lax.ppermute(grad, "pipe", swap)
            if step > 0 and p + 1 < pairs:
                source = sections - 2 - 2 * p
                below.append(lax.ppermute(grad, "pipe", [(source, source - 1)]))
            grads.append(grad)
            deltas.append(delta)
        from_above = below
        all_deltas += deltas
        all_grads.append(grads)

    sketch = pl.pallas_call(
        functools.partial(sketch_kernel, count=count, pairs=pairs, scale=scale),
        out_shape=jax.ShapeDtypeStruct((slots, micro, rank // 2, 2 * rank), BF16),
        in_specs=[SMEM] + [VMEM] * (len(all_deltas) + 2),
        out_specs=VMEM,
        compiler_params=PARAMS,
        name="sketch",
    )(places[0], *all_deltas, dense_g, act_sums)
    sketch = all_sum(sketch, ("dp", "tensor")).reshape(slots, micro, rank * rank)

    picked = []
    for step in range(count + 1):
        value = all_grads[0][step]
        for p in range(1, pairs):
            value = jnp.where(pair == pairs - 1 - p, all_grads[p][step], value)
        picked.append(value)
    segment_out = jnp.concatenate([jnp.where(odd == 1, picked[c], picked[c + 1]) for c in range(count)])
    return (segment_out[None], sketch[None])


def solution(mesh):
    return jax.shard_map(
        shards,
        mesh=mesh,
        in_specs=(
            P(None, "dp", "tensor"),
            P("pipe", None, None, "dp", "tensor"),
            P("pipe", None, "tensor", None, None),
            P("pipe", None, None, None, None),
            P("pipe", None, None),
            P(),
        ),
        out_specs=(P("pipe", None, "dp", "tensor"), P("pipe", None, None, None)),
        check_vma=False,
    )
```

```python
import functools
import math

import jax
import jax.numpy as jnp
from jax import lax
from jax.experimental import pallas as pl
from jax.experimental.pallas import tpu as pltpu
from jax.sharding import PartitionSpec as P

F32 = jnp.float32
BF16 = jnp.bfloat16
VMEM = pl.BlockSpec(memory_space=pltpu.VMEM)
SMEM = pl.BlockSpec(memory_space=pltpu.SMEM)
ANY = pl.BlockSpec(memory_space=pl.ANY)
PARAMS = pltpu.CompilerParams(vmem_limit_bytes=16 * 1024 * 1024)
NN = (((1,), (0,)), ((), ()))
NT = (((1,), (1,)), ((), ()))


def mm(a, b, dims=NN):
    return lax.dot_general(a, b, dims, preferred_element_type=F32)


def silu_slope(value):
    sig = 0.5 + 0.5 * jnp.tanh(0.5 * value)
    return sig * (1.0 + value * (1.0 - sig))


def left_lanes(shape, rank):
    return lax.broadcasted_iota(jnp.int32, shape, len(shape) - 1) < rank


def head_lanes(h, head_size):
    return slice(h * head_size, (h + 1) * head_size)


def slopes_of(k, at, acts, mixing, slopes):
    chunk, tokens, width = slopes.shape[1:]
    heads, head_size = mixing.shape[1], mixing.shape[2]
    pre = []
    for h in range(heads):
        act = acts[k, at : at + chunk, :, head_lanes(h, head_size)].reshape(chunk * tokens, head_size)
        pre.append(mm(act, mixing[k, h]))
    for h in range(heads):
        slopes[k, :, :, head_lanes(h, head_size)] = silu_slope(pre[h]).reshape(chunk, tokens, head_size)


def chain(live, source, slopes, mixing, grad, deltas):
    chunk, tokens, width = grad.shape
    heads, head_size = mixing.shape[1], mixing.shape[2]
    rows = chunk * tokens
    grad[...] = source

    def slot(i, _):
        k = live - 1 - i
        old, delta = [], []
        for h in range(heads):
            lanes = head_lanes(h, head_size)
            g = grad[:, :, lanes].reshape(rows, head_size).astype(F32)
            old.append(g)
            delta.append((g * slopes[k, :, :, lanes].reshape(rows, head_size)).astype(BF16))
        back = [mm(delta[h], mixing[k, h], NT) for h in range(heads)]
        for h in range(heads):
            lanes = head_lanes(h, head_size)
            deltas[k, :, :, lanes] = delta[h].reshape(chunk, tokens, head_size)
            grad[:, :, lanes] = (old[h] + back[h]).astype(BF16).reshape(chunk, tokens, head_size)
        return 0

    lax.fori_loop(0, live, slot, 0)


def here(pair):
    section = lax.axis_index("pipe")
    return section // 2 == pair, section % 2 == 1


def first_kernel(pair, sizes, top, acts, mixing, grad, deltas, slopes, acts_v, mixing_v, top_v, sems):
    slots = acts.shape[0]
    chunk, micro = grad.shape[0], acts.shape[1]
    section = lax.axis_index("pipe")
    live = sizes[section]
    copies = []

    def load(src, dst):
        copy = pltpu.make_async_copy(src, dst, sems.at[len(copies)])
        copy.start()
        copies.append(copy)
        return copy

    need = {}
    for k in range(slots - 1, -1, -1):
        need[k] = (
            load(mixing.at[k], mixing_v.at[k]),
            load(acts.at[k, pl.ds(0, chunk)], acts_v.at[k, pl.ds(0, chunk)]),
        )
    first = load(top.at[pl.ds(0, chunk)], top_v.at[pl.ds(0, chunk)])
    rest = [load(acts.at[k, pl.ds(chunk, micro - chunk)], acts_v.at[k, pl.ds(chunk, micro - chunk)]) for k in range(slots)]
    rest.append(load(top.at[pl.ds(chunk, micro - chunk)], top_v.at[pl.ds(chunk, micro - chunk)]))
    for k in range(slots - 1, -1, -1):
        for copy in need[k]:
            copy.wait()

        @pl.when(k < live)
        def _():
            slopes_of(k, 0, acts_v, mixing_v, slopes)

    first.wait()
    active, odd = here(pair)

    @pl.when(jnp.logical_and(active, odd))
    def _():
        chain(live, top_v[:chunk], slopes, mixing_v, grad, deltas)

    for copy in rest:
        copy.wait()


def slope_kernel(at, sizes, acts, mixing, slopes):
    section = lax.axis_index("pipe")
    live = sizes[section]

    for k in range(acts.shape[0]):

        @pl.when(k < live)
        def _():
            slopes_of(k, at, acts, mixing, slopes)


def chain_kernel(pair, odd_at, has_odd, has_even, sizes, mixing, *refs):
    refs = list(refs)
    odd_in, odd_slopes = (refs.pop(0), refs.pop(0)) if has_odd else (None, None)
    even_in, even_slopes = (refs.pop(0), refs.pop(0)) if has_even else (None, None)
    grad, deltas = refs
    chunk = grad.shape[0]
    section = lax.axis_index("pipe")
    live = sizes[section]
    active, odd = here(pair)

    if has_odd:

        @pl.when(jnp.logical_and(active, odd))
        def _():
            chain(live, odd_in[odd_at : odd_at + chunk], odd_slopes, mixing, grad, deltas)

    if has_even:

        @pl.when(jnp.logical_and(active, jnp.logical_not(odd)))
        def _():
            chain(live, even_in[...], even_slopes, mixing, grad, deltas)


def prep_kernel(blocks, tiles, acts, dense_g, act_sums, dense_a):
    slots, picks, head_size, both = tiles.shape
    rank = both // 2
    micro = acts.shape[1]
    heads = dense_a.shape[1] // head_size
    first_head = lax.axis_index("tensor") * heads
    row = lax.broadcasted_iota(jnp.int32, (both, both), 0)
    col = lax.broadcasted_iota(jnp.int32, (both, both), 1)
    twice = (row == col % rank).astype(BF16)
    row = lax.broadcasted_iota(jnp.int32, (rank, both), 0)
    col = lax.broadcasted_iota(jnp.int32, (rank, both), 1)
    split = (col == rank + jnp.where(row < rank // 2, 2 * row, 2 * row - rank + 1)).astype(BF16)
    dense_a[...] = jnp.zeros_like(dense_a)
    dense_g[...] = jnp.zeros_like(dense_g)
    for k in range(slots):
        for j in range(picks):
            own = blocks[k, j] - first_head

            @pl.when(jnp.logical_and(own >= 0, own < heads))
            def _():
                place = pl.ds(pl.multiple_of(own * head_size, head_size), head_size)
                tile = tiles[k, j]
                dense_a[k, place, :] = mm(tile, twice).astype(BF16)
                dense_g[k, :, place] = mm(split, tile, NT).astype(BF16)

    half = micro // 2
    tokens = acts.shape[2]

    def project(k, _):
        one = mm(acts[k, :half].reshape(half * tokens, -1), dense_a[k])
        two = mm(acts[k, half:].reshape(half * tokens, -1), dense_a[k])
        act_sums[k] = jnp.where(left_lanes(one.shape, rank), one, two).astype(BF16)
        return 0

    lax.fori_loop(0, slots, project, 0)


def sketch_kernel(chunks, pairs, scale, sizes, *refs):
    per = len(chunks) + 1
    deltas = [refs[p * per : (p + 1) * per] for p in range(pairs)]
    dense_g, act_sums, out = refs[pairs * per :]
    slots, chunk, tokens, width = deltas[0][0].shape
    rank = dense_g.shape[1]
    both = 2 * rank
    rows = chunk * tokens
    half = act_sums.shape[1]
    section = lax.axis_index("pipe")
    live = sizes[section]

    def one(ref, i):
        start = chunks[i] * rows
        token = lax.broadcasted_iota(jnp.int32, (rows, both), 0) // tokens
        for k in range(slots):

            @pl.when(k < live)
            def _():
                proj = mm(dense_g[k], ref[k].reshape(rows, width), NT).astype(BF16)
                act = act_sums[k, start % half : start % half + rows]
                other = pltpu.roll(act, rank, 1)
                left = left_lanes(act.shape, rank)
                act = jnp.where(left, act, other) if start < half else jnp.where(left, other, act)
                spread = jnp.concatenate([jnp.where(token == m, act, 0.0) for m in range(chunk)], axis=1)
                full = mm(proj, spread.astype(BF16))
                for m in range(chunk):
                    even = full[: rank // 2, m * both : (m + 1) * both]
                    uneven = full[rank // 2 :, m * both : (m + 1) * both]
                    res = jnp.where(left_lanes(even.shape, rank), even, uneven) * scale
                    out[k, i * chunk + m] = res.astype(BF16)

            @pl.when(k >= live)
            def _():
                out[k, i * chunk : (i + 1) * chunk] = jnp.zeros((chunk, rank // 2, both), BF16)

    for i in range(len(chunks)):
        for p in range(pairs):
            active, odd = here(pairs - 1 - p)

            @pl.when(jnp.logical_and(active, odd))
            def _():
                one(deltas[p][i], i)

            @pl.when(jnp.logical_and(active, jnp.logical_not(odd)))
            def _():
                one(deltas[p][i + 1], i)


def swap_sum(x, axis, by):
    peers = lax.axis_size(axis)
    other = lax.ppermute(x, axis, [(i, i ^ by) for i in range(peers)])
    return x.astype(F32) + other.astype(F32)


def all_sum(x, axes):
    x = x.astype(BF16)
    total = x.astype(F32)
    for axis in axes:
        peers = lax.axis_size(axis)
        if peers & (peers - 1):
            total = lax.psum(total, axis)
        else:
            by = 1
            while by < peers:
                total = swap_sum(total.astype(BF16), axis, by)
                by *= 2
    return total


def shards(grad_out, activations, mixing, proj_tiles, proj_blocks, section_sizes):
    sections = lax.axis_size("pipe")
    section = lax.axis_index("pipe")
    micro, tokens, width = grad_out.shape
    slots = activations.shape[1]
    rank = proj_tiles.shape[4] // 2
    scale = 1.0 / math.sqrt(tokens * lax.axis_size("dp"))
    pairs = sections // 2
    count = 4
    chunk = micro // count
    pair = section // 2

    def call(kernel, name, ins, specs, outs, scratch=()):
        outs = tuple(jax.ShapeDtypeStruct(s, t) for s, t in outs)
        return pl.pallas_call(
            kernel,
            out_shape=outs,
            in_specs=specs,
            out_specs=(VMEM,) * len(outs),
            scratch_shapes=scratch,
            compiler_params=PARAMS,
            name=name,
        )(*ins)

    step_outs = [((chunk, tokens, width), BF16), ((slots, chunk, tokens, width), BF16)]
    slope_out = ((slots, chunk, tokens, width), F32)
    grad, delta, slope, acts, mix, top = call(
        functools.partial(first_kernel, pairs - 1),
        "first",
        (section_sizes, grad_out, activations[0], mixing[0]),
        [SMEM, ANY, ANY, ANY],
        step_outs
        + [slope_out, (activations.shape[1:], BF16), (mixing.shape[1:], BF16), (grad_out.shape, BF16)],
        [pltpu.SemaphoreType.DMA((3 * slots + 2,))],
    )
    slopes = [slope]

    swap = [(i, i ^ 1) for i in range(sections)]
    from_above = [(top, c * chunk) for c in range(count)]
    all_deltas, all_grads = [], []
    for p in range(pairs):
        deltas, grads, below = [], [], []
        even_in = None
        for step in range(count + 1):
            if p > 0 or step > 0:
                ins, specs = [section_sizes, mix], [SMEM, VMEM]
                has_odd, has_even = step < count, step > 0
                odd_at = 0
                if has_odd:
                    source, odd_at = from_above[step]
                    ins += [source, slopes[step]]
                if has_even:
                    ins += [even_in, slopes[step - 1]]
                specs += [VMEM] * (len(ins) - 2)
                kernel = functools.partial(chain_kernel, pairs - 1 - p, odd_at, has_odd, has_even)
                grad, delta = call(kernel, "chain", ins, specs, step_outs)
            if step < count:
                even_in = lax.ppermute(grad, "pipe", swap)
            if step > 0 and p + 1 < pairs:
                source = sections - 2 - 2 * p
                below.append((lax.ppermute(grad, "pipe", [(source, source - 1)]), 0))
            grads.append(grad)
            deltas.append(delta)
            if p == 0 and step + 1 < count:
                slopes += call(
                    functools.partial(slope_kernel, (step + 1) * chunk),
                    "slope",
                    (section_sizes, acts, mix),
                    [SMEM, VMEM, VMEM],
                    [slope_out],
                )
        from_above = below
        all_deltas.append(deltas)
        all_grads.append(grads)

    dense_g, act_part = call(
        prep_kernel,
        "prep",
        (proj_blocks[0], proj_tiles[0], acts),
        [SMEM, VMEM, VMEM],
        [((slots, rank, width), BF16), ((slots, micro // 2 * tokens, 2 * rank), BF16)],
        [pltpu.VMEM((slots, width, 2 * rank), BF16)],
    )
    act_sums = all_sum(act_part, ("tensor",))

    parts = []
    for chunks in (range(0, count // 2), range(count // 2, count)):
        ins = [section_sizes]
        for deltas in all_deltas:
            ins += deltas[chunks[0] : chunks[-1] + 2]
        ins += [dense_g, act_sums]
        (part,) = call(
            functools.partial(sketch_kernel, list(chunks), pairs, scale),
            "sketch",
            ins,
            [SMEM] + [VMEM] * (len(ins) - 1),
            [((slots, len(chunks) * chunk, rank // 2, 2 * rank), BF16)],
        )
        parts.append(all_sum(part, ("dp", "tensor")))
    sketch = jnp.concatenate(parts, axis=1).reshape(slots, micro, rank * rank)

    picked = []
    for step in range(count + 1):
        value = all_grads[0][step]
        for p in range(1, pairs):
            value = jnp.where(pair == pairs - 1 - p, all_grads[p][step], value)
        picked.append(value)
    segment_out = jnp.concatenate([jnp.where(section % 2 == 1, picked[c], picked[c + 1]) for c in range(count)])
    return (segment_out[None], sketch[None])


def solution(mesh):
    return jax.shard_map(
        shards,
        mesh=mesh,
        in_specs=(
            P(None, "dp", "tensor"),
            P("pipe", None, None, "dp", "tensor"),
            P("pipe", None, "tensor", None, None),
            P("pipe", None, None, None, None),
            P("pipe", None, None),
            P(),
        ),
        out_specs=(P("pipe", None, "dp", "tensor"), P("pipe", None, None, None)),
        check_vma=False,
    )
```

```python
import functools
import math

import jax
import jax.numpy as jnp
from jax import lax
from jax.experimental import pallas as pl
from jax.experimental.pallas import tpu as pltpu
from jax.sharding import PartitionSpec as P

F32 = jnp.float32
BF16 = jnp.bfloat16
VMEM = pl.BlockSpec(memory_space=pltpu.VMEM)
HBM = pl.BlockSpec(memory_space=pltpu.HBM)
PARAMS = pltpu.CompilerParams(vmem_limit_bytes=16 * 1024 * 1024)
NN = (((1,), (0,)), ((), ()))
NT = (((1,), (1,)), ((), ()))
TN = (((0,), (0,)), ((), ()))
FLAG = (8, 128)
LIGHT = 1000
WORK = (1000, 1000, 300, 10000, 2000, 2000, 2000, 10000, 3000, 2000, 6000, 10000, 3000, 6000, 3000, 1, 3000, 10000, 3000, 1000, 2000, 6000, 6000, 6000, 300, 1000, 2000, 1000, 3000)


def mm(a, b, dims=NN):
    return lax.dot_general(a, b, dims, preferred_element_type=F32)


def silu_slope(value):
    sig = 0.5 + 0.5 * jnp.tanh(0.5 * value)
    return sig * (1.0 + value * (1.0 - sig))


def left_lanes(shape, rank):
    return lax.broadcasted_iota(jnp.int32, shape, len(shape) - 1) < rank


def head_lanes(h, head_size):
    return slice(h * head_size, (h + 1) * head_size)


def live_slots(info):
    return jnp.max(info[...]).astype(jnp.int32)


def here(pair):
    section = lax.axis_index("pipe")
    return section // 2 == pair, section % 2 == 1


def slopes_of(k, at, acts, mix_act, slopes, part=None):
    chunk, tokens, width = slopes.shape[1:]
    heads, head_size = mix_act.shape[1], mix_act.shape[2]
    rows = chunk * tokens
    total = 0.0
    for h in range(heads):
        act = acts[k, at : at + chunk, :, head_lanes(h, head_size)].reshape(rows, head_size)
        if part is None:
            pre = mm(act, mix_act[k, h, :, :head_size])
        else:
            both = mm(act, mix_act[k, h])
            total += both[:, head_size:]
            pre = both[:, :head_size]
        slope = silu_slope(pre).astype(slopes.dtype)
        slopes[k, :, :, head_lanes(h, head_size)] = slope.reshape(chunk, tokens, head_size)
    if part is not None:
        part[k] = total.astype(BF16)


def project_of(k, at, chunk, acts, mix_act):
    tokens = acts.shape[2]
    heads, head_size = mix_act.shape[1], mix_act.shape[2]
    total = 0.0
    for h in range(heads):
        act = acts[k, at : at + chunk, :, head_lanes(h, head_size)].reshape(chunk * tokens, head_size)
        total += mm(act, mix_act[k, h, :, head_size:])
    return total


def chain(live, source, slopes, mix_grad, grad, proj):
    chunk, tokens, width = grad.shape
    heads, head_size = mix_grad.shape[1], mix_grad.shape[3]
    rows = chunk * tokens
    grad[...] = source

    def slot(i, _):
        k = live - 1 - i
        old, both = [], []
        for h in range(heads):
            lanes = head_lanes(h, head_size)
            g = grad[:, :, lanes].reshape(rows, head_size).astype(F32)
            delta = (g * slopes[k, :, :, lanes].reshape(rows, head_size).astype(F32)).astype(BF16)
            old.append(g)
            both.append(mm(delta, mix_grad[k, h], NT))
        total = jnp.zeros((rows, proj.shape[2]), F32)
        for h in range(heads):
            lanes = head_lanes(h, head_size)
            grad[:, :, lanes] = (old[h] + both[h][:, :head_size]).astype(BF16).reshape(chunk, tokens, head_size)
            total += both[h][:, head_size:]
        proj[k] = total.astype(BF16)
        return 0

    lax.fori_loop(0, live, slot, 0)


def spread_tiles(k, blocks, tiles, mix_act, mix_grad):
    picks, head_size, both = tiles.shape[1:]
    rank = both // 2
    heads = mix_act.shape[1]
    first_head = lax.axis_index("tensor") * heads
    row = lax.broadcasted_iota(jnp.int32, (both, both), 0)
    col = lax.broadcasted_iota(jnp.int32, (both, both), 1)
    twice = (row == col % rank).astype(BF16)
    order = rank + jnp.where(row < rank // 2, 2 * row, 2 * row - rank + 1)
    split = jnp.logical_and(col == order, row < rank).astype(BF16)
    mix_act[k, :, :, head_size:] = jnp.zeros((heads, head_size, both), BF16)
    mix_grad[k, :, head_size:, :] = jnp.zeros((heads, both, head_size), BF16)
    for j in range(picks):
        own = blocks[k, 0, j] - first_head

        @pl.when(jnp.logical_and(own >= 0, own < heads))
        def _():
            tile = tiles[k, j]
            mix_act[k, own, :, head_size:] = mm(tile, twice).astype(BF16)
            mix_grad[k, own, head_size:, :] = mm(split, tile, NT).astype(BF16)


def first_kernel(
    pair, sizes_in, blocks_in, top, acts, mixing, tiles,
    grad, proj, slopes, part, next_slopes, next_part, acts_v, top_v, mix_act, mix_grad, info,
    sizes, blocks, tiles_v, sems,
):
    slots = acts.shape[0]
    head_size = mixing.shape[2]
    chunk, micro = grad.shape[0], acts.shape[1]
    copies = []

    def load(src, dst):
        copy = pltpu.make_async_copy(src, dst, sems.at[len(copies)])
        copy.start()
        copies.append(copy)
        return copy

    order = range(slots - 1, -1, -1)
    scalars = (load(sizes_in, sizes), load(blocks_in, blocks))
    spread = {k: load(tiles.at[k], tiles_v.at[k]) for k in order}
    need = {
        k: (
            load(mixing.at[k], mix_act.at[k, :, :, pl.ds(0, head_size)]),
            load(acts.at[k, pl.ds(0, chunk)], acts_v.at[k, pl.ds(0, chunk)]),
        )
        for k in order
    }
    first = [load(mixing.at[k], mix_grad.at[k, :, pl.ds(0, head_size), :]) for k in order]
    first.append(load(top.at[pl.ds(0, chunk)], top_v.at[pl.ds(0, chunk)]))
    second = [load(acts.at[k, pl.ds(chunk, chunk)], acts_v.at[k, pl.ds(chunk, chunk)]) for k in order]
    left = micro - 2 * chunk
    rest = [load(acts.at[k, pl.ds(2 * chunk, left)], acts_v.at[k, pl.ds(2 * chunk, left)]) for k in order]
    rest.append(load(top.at[pl.ds(chunk, micro - chunk)], top_v.at[pl.ds(chunk, micro - chunk)]))
    for copy in scalars:
        copy.wait()
    live = sizes[lax.axis_index("pipe")]
    info[...] = jnp.full(info.shape, live.astype(F32))
    for k in order:
        spread[k].wait()
        pl.when(k < live)(functools.partial(spread_tiles, k, blocks, tiles_v, mix_act, mix_grad))
    for k in order:
        for copy in need[k]:
            copy.wait()
        pl.when(k < live)(functools.partial(slopes_of, k, 0, acts_v, mix_act, slopes, part))
    for copy in first + second:
        copy.wait()
    active, odd = here(pair)
    ahead = jnp.logical_and(active, odd)

    @pl.when(ahead)
    def _():
        chain(live, top_v[:chunk], slopes, mix_grad, grad, proj)

    for k in order:
        pl.when(jnp.logical_and(k < live, jnp.logical_not(ahead)))(
            functools.partial(slopes_of, k, chunk, acts_v, mix_act, next_slopes, next_part)
        )
    for copy in rest:
        copy.wait()


def lay(act_part, group, k, one, two):
    left = left_lanes(one.shape, one.shape[1] // 2)
    act_part[group, k] = jnp.where(left, one, two).astype(BF16)


def beside_kernel(pair, info, acts, mix_act, after, first_part, second_part, slopes, act_part, token, part):
    chunk = slopes.shape[1]
    live = live_slots(info)
    active, odd = here(pair)
    ahead = jnp.logical_and(active, odd)
    for k in range(acts.shape[0]):

        @pl.when(jnp.logical_and(k < live, ahead))
        def _():
            both = project_of(k, 2 * chunk, 2 * chunk, acts, mix_act)
            half = both.shape[0] // 2
            lay(act_part, 1, k, both[:half], both[half:])

        @pl.when(jnp.logical_and(k < live, jnp.logical_not(ahead)))
        def _():
            slopes_of(k, 2 * chunk, acts, mix_act, slopes, part)
            lay(act_part, 0, k, first_part[k], second_part[k])
            lay(act_part, 1, k, part[k], project_of(k, 3 * chunk, chunk, acts, mix_act))


def slope_kernel(pair, at, info, acts, mix_act, after, slopes, token):
    live = live_slots(info)
    active, odd = here(pair)
    ahead = jnp.logical_and(active, odd)
    for k in range(acts.shape[0]):
        pl.when(jnp.logical_and(k < live, jnp.logical_not(ahead)))(
            functools.partial(slopes_of, k, at, acts, mix_act, slopes)
        )


def top_kernel(pair, at, has_odd, info, mix_grad, after, even_in, even_slopes, *refs):
    refs = list(refs)
    top, acts, mix_act = (refs.pop(0), refs.pop(0), refs.pop(0)) if has_odd else (None, None, None)
    first_part, _ = (refs.pop(0), refs.pop(0)) if at == 1 else (None, None)
    grad, proj, token = refs[:3]
    refs = refs[3:]
    act_part = refs.pop(0) if at == 1 else None
    slopes = refs.pop(0) if has_odd else None
    part = refs.pop(0) if at == 1 else None
    active, odd = here(pair)

    @pl.when(jnp.logical_and(active, jnp.logical_not(odd)))
    def _():
        chain(live_slots(info), even_in[...], even_slopes, mix_grad, grad, proj)

    if has_odd:
        chunk = grad.shape[0]

        @pl.when(jnp.logical_and(active, odd))
        def _():
            live = live_slots(info)
            for k in range(acts.shape[0] - 1, -1, -1):

                @pl.when(k < live)
                def _():
                    slopes_of(k, at * chunk, acts, mix_act, slopes, part)
                    if at == 1:
                        lay(act_part, 0, k, first_part[k], part[k])

            chain(live, top[at * chunk : (at + 1) * chunk], slopes, mix_grad, grad, proj)


def step_kernel(pair, parity, info, mix_grad, after, source, slopes, grad, proj, token):
    active, odd = here(pair)

    @pl.when(jnp.logical_and(active, odd if parity else jnp.logical_not(odd)))
    def _():
        chain(live_slots(info), source[...], slopes, mix_grad, grad, proj)


def take_kernel(group, mine, other, after, total, token):
    total[...] = (mine[group].astype(F32) + other[group].astype(F32)).astype(total.dtype)


def widen_kernel(chunk, mine, other, after, out, token):
    slots, rows, both = mine.shape
    rank = both // 2
    batch = lax.broadcasted_iota(jnp.int32, (rows, both), 0) // (rows // chunk)
    left = left_lanes((rows, both), rank)
    for k in range(slots):
        act = mine[k].astype(F32) + other[k].astype(F32)
        swapped = pltpu.roll(act, rank, 1)
        for i in range(2):
            one = jnp.where(left, swapped, act) if i else jnp.where(left, act, swapped)
            for m in range(chunk):
                out[k, i, :, m * both : (m + 1) * both] = jnp.where(batch == m, one, 0.0).astype(BF16)


def add_kernel(mine, other, after, total, token):
    total[...] = (mine[...].astype(F32) + other[...].astype(F32)).astype(total.dtype)


def sketch_kernel(pairs, scale, info, after, *refs):
    projs = [refs[p * 4 : (p + 1) * 4] for p in range(pairs)]
    acts, out, token = refs[pairs * 4 :]
    slots, rows, both = projs[0][0].shape
    rank = both // 2
    chunk = out.shape[1] // 2
    live = live_slots(info)

    def one(ref, i):
        lower = left_lanes((rank // 2, both), rank)
        for k in range(slots):

            @pl.when(k < live)
            def _():
                full = mm(ref[k], acts[k, i], TN)
                for m in range(chunk):
                    even = full[: rank // 2, m * both : (m + 1) * both]
                    uneven = full[rank // 2 : rank, m * both : (m + 1) * both]
                    out[k, i * chunk + m] = (jnp.where(lower, even, uneven) * scale).astype(BF16)

            @pl.when(k >= live)
            def _():
                out[k, i * chunk : (i + 1) * chunk] = jnp.zeros((chunk, rank // 2, both), BF16)

    for p in range(pairs):
        active, odd = here(pairs - 1 - p)

        @pl.when(jnp.logical_and(active, odd))
        def _():
            for i in range(2):
                one(projs[p][i], i)

        @pl.when(jnp.logical_and(active, jnp.logical_not(odd)))
        def _():
            for i in range(2):
                one(projs[p][2 + i], i)


def collect_kernel(pairs, after, *refs):
    out, token = refs[-2:]
    count = (len(refs) - 2) // (2 * pairs)
    chunk = refs[0].shape[0]
    for p in range(pairs):
        active, odd = here(pairs - 1 - p)
        for parity in (1, 0):

            @pl.when(jnp.logical_and(active, odd if parity else jnp.logical_not(odd)))
            def _():
                for c in range(count):
                    out[c * chunk : (c + 1) * chunk] = refs[(2 * p + 1 - parity) * count + c][...]


def last_kernel(after, *refs):
    out = refs[-1]
    groups = [(refs[i], refs[i + 1]) for i in range(0, len(refs) - 1, 2)]
    slots, micro, parts, lanes = groups[0][0].shape
    for k in range(slots):
        total = jnp.concatenate([mine[k].astype(F32) + other[k].astype(F32) for mine, other in groups])
        total = jnp.swapaxes(total, 0, 1)
        for i in range(parts):
            out[k, :, i * lanes : (i + 1) * lanes] = total[i]


def swaps(axes):
    for axis in axes:
        peers = lax.axis_size(axis)
        if peers & (peers - 1):
            yield axis, 0
        else:
            by = 1
            while by < peers:
                yield axis, by
                by *= 2


def exchange(x, axis, by):
    if not by:
        return lax.psum(x.astype(F32), axis).astype(BF16) - x
    return lax.ppermute(x, axis, [(i, i ^ by) for i in range(lax.axis_size(axis))])


def shards(grad_out, activations, mixing, proj_tiles, proj_blocks, section_sizes):
    sections = lax.axis_size("pipe")
    section = lax.axis_index("pipe")
    micro, tokens, width = grad_out.shape
    slots = activations.shape[1]
    heads, head_size = mixing.shape[2:4]
    both = proj_tiles.shape[4]
    rank = both // 2
    scale = 1.0 / math.sqrt(tokens * lax.axis_size("dp"))
    pairs = sections // 2
    count = 4
    chunk = micro // count
    rows = chunk * tokens
    top_pair = pairs - 1
    last = None
    weights = iter(WORK)

    def call(kernel, name, ins, specs, outs, scratch=(), work=LIGHT, alias={}):
        outs = tuple(jax.ShapeDtypeStruct(s, t) for s, t in outs)
        return pl.pallas_call(
            kernel,
            out_shape=outs,
            in_specs=specs,
            out_specs=(VMEM,) * len(outs),
            scratch_shapes=scratch,
            input_output_aliases=alias,
            compiler_params=PARAMS,
            cost_estimate=pl.CostEstimate(flops=work, bytes_accessed=1000, transcendentals=0),
            name=name,
        )(*ins)

    def in_turn(kernel, name, first, ins, outs, more=(), scratch=(), work=LIGHT, alias=None):
        nonlocal last
        work = 10**6 * next(weights, 1)
        ins = [*first, last, *ins]
        res = call(kernel, name, ins, [VMEM] * len(ins), [*outs, (FLAG, F32), *more], scratch, work, alias or {})
        last = res[len(outs)]
        return [*res[: len(outs)], *res[len(outs) + 1 :]]

    step_outs = [((chunk, tokens, width), BF16), ((slots, rows, both), BF16)]
    slope_out = ((slots, chunk, tokens, width), F32)
    part_out = ((slots, rows, both), BF16)
    grad, proj, slope, part, next_slope, next_part, acts, top, mix_act, mix_grad, info = call(
        functools.partial(first_kernel, top_pair),
        "first",
        [
            pltpu.with_memory_space_constraint(x, pltpu.HBM)
            for x in (section_sizes, proj_blocks.transpose(1, 0, 2), grad_out, activations[0], mixing[0], proj_tiles[0])
        ],
        [HBM] * 6,
        [
            *step_outs,
            slope_out,
            part_out,
            slope_out,
            part_out,
            (activations.shape[1:], BF16),
            (grad_out.shape, BF16),
            ((slots, heads, head_size, head_size + both), BF16),
            ((slots, heads, head_size + both, head_size), BF16),
            (FLAG, F32),
        ],
        [
            pltpu.SMEM(section_sizes.shape, jnp.int32),
            pltpu.SMEM((slots, 1, proj_blocks.shape[2]), jnp.int32),
            pltpu.VMEM(proj_tiles.shape[1:], BF16),
            pltpu.SemaphoreType.DMA((6 * slots + 4,)),
        ],
    )
    last = info
    slopes = [slope, next_slope]
    swap = [(i, i ^ 1) for i in range(sections)]
    grads = [([], []) for _ in range(pairs)]
    projs = [([], []) for _ in range(pairs)]
    hops = [[] for _ in range(pairs)]
    core = [[] for _ in range(pairs)]

    def keep(p, odd, even, grad, proj):
        for parity, there in ((0, even), (1, odd)):
            if there:
                grads[p][parity].append(grad)
                projs[p][parity].append(proj)
        if odd:
            core[p].append(lax.ppermute(grad, "pipe", swap))
        if even and p + 1 < pairs:
            source = sections - 2 - 2 * p
            hops[p].append(lax.ppermute(grad, "pipe", [(source, source - 1)]))

    def top_step(at):
        ins, more, scratch, alias = [core[0][at - 1], slopes[at - 1]], [], [], {}
        if at < count:
            ins += [top, acts, mix_act]
            scratch.append(pltpu.VMEM(slope_out[0], F32))
        if at == 1:
            ins += [part, act_part]
            alias = {3 + len(ins) - 1: 3}
            more.append((act_part.shape, BF16))
            scratch.append(pltpu.VMEM(*part_out))
        kernel = functools.partial(top_kernel, top_pair, at, at < count)
        grad, proj, *rest = in_turn(kernel, "top", [info, mix_grad], ins, step_outs, more, scratch, alias=alias)
        keep(0, at < count, True, grad, proj)
        return rest

    def step(p, parity, at):
        source = hops[p - 1][at] if parity else core[p][at]
        kernel = functools.partial(step_kernel, top_pair - p, parity)
        keep(p, parity, not parity, *in_turn(kernel, "step", [info, mix_grad], [source, slopes[at]], step_outs))

    class Sum:
        def __init__(self, value, turns):
            self.mine, self.turns = value, turns
            self.go()

        def go(self):
            self.other = exchange(self.mine, *self.turns.pop(0))

        def turn(self, work=LIGHT):
            self.mine = in_turn(add_kernel, "add", [self.mine, self.other], [], [(self.mine.shape, BF16)], work=work)[0]
            self.go()

    def take(group, work=LIGHT):
        kernel = functools.partial(take_kernel, group)
        mine = in_turn(kernel, "take", [act_part, act_other], [], [part_out], work=work)[0]
        return Sum(mine, list(act_turns[1:]))

    def collect():
        ins = [grad for pair in grads for parity in (1, 0) for grad in pair[parity]]
        return in_turn(functools.partial(collect_kernel, pairs), "collect", [], ins, [(grad_out.shape, BF16)])[0]

    def sketch(group, act_sum):
        while act_sum.turns:
            act_sum.turn()
        out = ((slots, 2, rows, chunk * both), BF16)
        wide = in_turn(functools.partial(widen_kernel, chunk), "widen", [act_sum.mine, act_sum.other], [], [out])[0]
        ins = []
        for p in range(pairs):
            for parity in (1, 0):
                ins += projs[p][parity][2 * group : 2 * group + 2]
        kernel = functools.partial(sketch_kernel, pairs, scale)
        out = ((slots, 2 * chunk, rank // 2, both), BF16)
        return in_turn(kernel, "sketch", [info], [*ins, wide], [out])[0]

    low = pairs - 1
    act_turns = list(swaps(("tensor",)))
    turns = list(swaps(("dp", "tensor")))
    keep(0, True, False, grad, proj)
    slope, act_part = in_turn(
        functools.partial(beside_kernel, top_pair),
        "beside",
        [info, acts, mix_act],
        [part, next_part],
        [slope_out, ((2, *part_out[0]), BF16)],
        scratch=[pltpu.VMEM(*part_out)],
    )
    slopes.append(slope)
    (act_part,) = top_step(1)
    act_other = exchange(act_part, *act_turns[0])
    top_step(2)
    kernel = functools.partial(slope_kernel, top_pair, 3 * chunk)
    slopes += in_turn(kernel, "slope", [info, acts, mix_act], [], [slope_out])
    top_step(3)
    early_acts = take(0)
    for p in range(1, pairs):
        step(p, 1, 0)
        if p == 1:
            top_step(count)
        else:
            step(p - 1, 0, 3)
        step(p, 1, 1)
        step(p, 0, 0)
        if p == 1:
            late_acts = take(1)
        step(p, 1, 2)
        step(p, 0, 1)
        if p < low:
            step(p, 1, 3)
            step(p, 0, 2)
    early = Sum(sketch(0, early_acts), list(turns))
    step(low, 1, 3)
    step(low, 0, 2)
    early.turn()
    step(low, 0, 3)
    late = Sum(sketch(1, late_acts), list(turns))
    segment_out = collect()
    while late.turns:
        if early.turns:
            early.turn()
        late.turn()
    ins = [last, early.mine, early.other, late.mine, late.other]
    (total,) = call(last_kernel, "last", ins, [VMEM] * 5, [((slots, micro, rank * rank), F32)])

    return (segment_out[None], total[None])


def solution(mesh):
    return jax.shard_map(
        shards,
        mesh=mesh,
        in_specs=(
            P(None, "dp", "tensor"),
            P("pipe", None, None, "dp", "tensor"),
            P("pipe", None, "tensor", None, None),
            P("pipe", None, None, None, None),
            P("pipe", None, None),
            P(),
        ),
        out_specs=(P("pipe", None, "dp", "tensor"), P("pipe", None, None, None)),
        check_vma=False,
    )
```

```python
import functools
import math

import jax
import jax.numpy as jnp
from jax import lax
from jax.experimental import pallas as pl
from jax.experimental.pallas import tpu as pltpu
from jax.sharding import PartitionSpec as P

F32 = jnp.float32
BF16 = jnp.bfloat16
VMEM = pl.BlockSpec(memory_space=pltpu.VMEM)
HBM = pl.BlockSpec(memory_space=pltpu.HBM)
PARAMS = pltpu.CompilerParams(vmem_limit_bytes=16 * 1024 * 1024)
NN = (((1,), (0,)), ((), ()))
NT = (((1,), (1,)), ((), ()))
TN = (((0,), (0,)), ((), ()))
FLAG = (8, 128)
LIGHT = 1000
WORK = (3000, 1000, 6000, 1000, 10000, 6000, 10000, 6000, 10000, 3000, 1, 10000, 2000, 10000, 300, 6000, 1, 300, 1, 10000, 2000, 10000, 3000, 2000, 3000, 1)


def mm(a, b, dims=NN):
    return lax.dot_general(a, b, dims, preferred_element_type=F32)


def silu_slope(value):
    sig = 0.5 + 0.5 * jnp.tanh(0.5 * value)
    return sig * (1.0 + value * (1.0 - sig))


def left_lanes(shape, rank):
    return lax.broadcasted_iota(jnp.int32, shape, len(shape) - 1) < rank


def head_lanes(h, head_size):
    return slice(h * head_size, (h + 1) * head_size)


def live_slots(info):
    return jnp.max(info[...]).astype(jnp.int32)


def here(pair):
    section = lax.axis_index("pipe")
    return section // 2 == pair, section % 2 == 1


def slopes_of(k, at, acts, mix_act, slopes, part=None):
    chunk, tokens, width = slopes.shape[1:]
    heads, head_size = mix_act.shape[1], mix_act.shape[2]
    rows = chunk * tokens
    total = 0.0
    for h in range(heads):
        act = acts[k, at : at + chunk, :, head_lanes(h, head_size)].reshape(rows, head_size)
        if part is None:
            pre = mm(act, mix_act[k, h, :, :head_size])
        else:
            both = mm(act, mix_act[k, h])
            total += both[:, head_size:]
            pre = both[:, :head_size]
        slope = silu_slope(pre).astype(slopes.dtype)
        slopes[k, :, :, head_lanes(h, head_size)] = slope.reshape(chunk, tokens, head_size)
    if part is not None:
        part[k] = total.astype(BF16)


def project_of(k, at, chunk, acts, mix_act):
    tokens = acts.shape[2]
    heads, head_size = mix_act.shape[1], mix_act.shape[2]
    total = 0.0
    for h in range(heads):
        act = acts[k, at : at + chunk, :, head_lanes(h, head_size)].reshape(chunk * tokens, head_size)
        total += mm(act, mix_act[k, h, :, head_size:])
    return total


def chain(live, source, slopes, mix_grad, grad, proj):
    chunk, tokens, width = grad.shape
    heads, head_size = mix_grad.shape[1], mix_grad.shape[3]
    rows = chunk * tokens
    grad[...] = source

    def slot(i, _):
        k = live - 1 - i
        old, both = [], []
        for h in range(heads):
            lanes = head_lanes(h, head_size)
            g = grad[:, :, lanes].reshape(rows, head_size).astype(F32)
            delta = (g * slopes[k, :, :, lanes].reshape(rows, head_size).astype(F32)).astype(BF16)
            old.append(g)
            both.append(mm(delta, mix_grad[k, h], NT))
        total = jnp.zeros((rows, proj.shape[2]), F32)
        for h in range(heads):
            lanes = head_lanes(h, head_size)
            grad[:, :, lanes] = (old[h] + both[h][:, :head_size]).astype(BF16).reshape(chunk, tokens, head_size)
            total += both[h][:, head_size:]
        proj[k] = total.astype(BF16)
        return 0

    lax.fori_loop(0, live, slot, 0)


def spread_tiles(k, blocks, tiles, mix_act, mix_grad):
    picks, head_size, both = tiles.shape[1:]
    rank = both // 2
    heads = mix_act.shape[1]
    first_head = lax.axis_index("tensor") * heads
    row = lax.broadcasted_iota(jnp.int32, (both, both), 0)
    col = lax.broadcasted_iota(jnp.int32, (both, both), 1)
    twice = (row == col % rank).astype(BF16)
    order = rank + jnp.where(row < rank // 2, 2 * row, 2 * row - rank + 1)
    split = jnp.logical_and(col == order, row < rank).astype(BF16)
    mix_act[k, :, :, head_size:] = jnp.zeros((heads, head_size, both), BF16)
    mix_grad[k, :, head_size:, :] = jnp.zeros((heads, both, head_size), BF16)
    for j in range(picks):
        own = blocks[k, 0, j] - first_head

        @pl.when(jnp.logical_and(own >= 0, own < heads))
        def _():
            tile = tiles[k, j]
            mix_act[k, own, :, head_size:] = mm(tile, twice).astype(BF16)
            mix_grad[k, own, head_size:, :] = mm(split, tile, NT).astype(BF16)


def first_kernel(
    pair, sizes_in, blocks_in, top, acts, mixing, tiles,
    grad, proj, slopes, part, next_slopes, next_part, acts_v, top_v, mix_act, mix_grad, info,
    sizes, blocks, tiles_v, sems,
):
    slots = acts.shape[0]
    head_size = mixing.shape[2]
    chunk, micro = grad.shape[0], acts.shape[1]
    copies = []

    def load(src, dst):
        copy = pltpu.make_async_copy(src, dst, sems.at[len(copies)])
        copy.start()
        copies.append(copy)
        return copy

    order = range(slots - 1, -1, -1)
    scalars = (load(sizes_in, sizes), load(blocks_in, blocks))
    spread = {k: load(tiles.at[k], tiles_v.at[k]) for k in order}
    need = {
        k: (
            load(mixing.at[k], mix_act.at[k, :, :, pl.ds(0, head_size)]),
            load(acts.at[k, pl.ds(0, chunk)], acts_v.at[k, pl.ds(0, chunk)]),
        )
        for k in order
    }
    first = [load(mixing.at[k], mix_grad.at[k, :, pl.ds(0, head_size), :]) for k in order]
    first.append(load(top.at[pl.ds(0, chunk)], top_v.at[pl.ds(0, chunk)]))
    second = [load(acts.at[k, pl.ds(chunk, chunk)], acts_v.at[k, pl.ds(chunk, chunk)]) for k in order]
    left = micro - 2 * chunk
    rest = [load(acts.at[k, pl.ds(2 * chunk, left)], acts_v.at[k, pl.ds(2 * chunk, left)]) for k in order]
    rest.append(load(top.at[pl.ds(chunk, micro - chunk)], top_v.at[pl.ds(chunk, micro - chunk)]))
    for copy in scalars:
        copy.wait()
    live = sizes[lax.axis_index("pipe")]
    info[...] = jnp.full(info.shape, live.astype(F32))
    for k in order:
        spread[k].wait()
        pl.when(k < live)(functools.partial(spread_tiles, k, blocks, tiles_v, mix_act, mix_grad))
    for k in order:
        for copy in need[k]:
            copy.wait()
        pl.when(k < live)(functools.partial(slopes_of, k, 0, acts_v, mix_act, slopes, part))
    for copy in first + second:
        copy.wait()
    active, odd = here(pair)
    ahead = jnp.logical_and(active, odd)

    @pl.when(ahead)
    def _():
        chain(live, top_v[:chunk], slopes, mix_grad, grad, proj)

    for k in order:
        pl.when(jnp.logical_and(k < live, jnp.logical_not(ahead)))(
            functools.partial(slopes_of, k, chunk, acts_v, mix_act, next_slopes, next_part)
        )
    for copy in rest:
        copy.wait()


def lay(act_part, group, k, one, two):
    left = left_lanes(one.shape, one.shape[1] // 2)
    act_part[group, k] = jnp.where(left, one, two).astype(BF16)


def beside_kernel(pair, info, acts, mix_act, after, first_part, second_part, slopes, act_part, token, part):
    chunk = slopes.shape[1]
    live = live_slots(info)
    active, odd = here(pair)
    ahead = jnp.logical_and(active, odd)
    for k in range(acts.shape[0]):

        @pl.when(jnp.logical_and(k < live, ahead))
        def _():
            rest = project_of(k, chunk, 3 * chunk, acts, mix_act)
            rows = rest.shape[0] // 3
            lay(act_part, 0, k, first_part[k], rest[:rows])
            lay(act_part, 1, k, rest[rows : 2 * rows], rest[2 * rows :])

        @pl.when(jnp.logical_and(k < live, jnp.logical_not(ahead)))
        def _():
            slopes_of(k, 2 * chunk, acts, mix_act, slopes, part)
            lay(act_part, 0, k, first_part[k], second_part[k])
            lay(act_part, 1, k, part[k], project_of(k, 3 * chunk, chunk, acts, mix_act))


def slope_kernel(pair, at, info, acts, mix_act, after, slopes, token):
    live = live_slots(info)
    active, odd = here(pair)
    ahead = jnp.logical_and(active, odd)
    for k in range(acts.shape[0]):
        pl.when(jnp.logical_and(k < live, jnp.logical_not(ahead)))(
            functools.partial(slopes_of, k, at, acts, mix_act, slopes)
        )


def top_kernel(pair, at, has_odd, info, mix_grad, after, even_in, even_slopes, *refs):
    refs = list(refs)
    top, acts, mix_act = (refs.pop(0), refs.pop(0), refs.pop(0)) if has_odd else (None, None, None)
    grad, proj, token = refs[:3]
    slopes = refs[3] if has_odd else None
    active, odd = here(pair)

    @pl.when(jnp.logical_and(active, jnp.logical_not(odd)))
    def _():
        chain(live_slots(info), even_in[...], even_slopes, mix_grad, grad, proj)

    if has_odd:
        chunk = grad.shape[0]

        @pl.when(jnp.logical_and(active, odd))
        def _():
            live = live_slots(info)
            for k in range(acts.shape[0] - 1, -1, -1):
                pl.when(k < live)(functools.partial(slopes_of, k, at * chunk, acts, mix_act, slopes))
            chain(live, top[at * chunk : (at + 1) * chunk], slopes, mix_grad, grad, proj)


def step_kernel(pair, parity, info, mix_grad, after, source, slopes, grad, proj, token):
    active, odd = here(pair)

    @pl.when(jnp.logical_and(active, odd if parity else jnp.logical_not(odd)))
    def _():
        chain(live_slots(info), source[...], slopes, mix_grad, grad, proj)


def widen_kernel(group, chunk, mine, other, after, out, token):
    slots, rows, both = mine.shape[1:]
    rank = both // 2
    batch = lax.broadcasted_iota(jnp.int32, (rows, both), 0) // (rows // chunk)
    left = left_lanes((rows, both), rank)
    for k in range(slots):
        act = mine[group, k].astype(F32) + other[group, k].astype(F32)
        swapped = pltpu.roll(act, rank, 1)
        for i in range(2):
            one = jnp.where(left, swapped, act) if i else jnp.where(left, act, swapped)
            for m in range(chunk):
                out[k, i, :, m * both : (m + 1) * both] = jnp.where(batch == m, one, 0.0).astype(BF16)


def add_kernel(mine, other, after, total, token):
    total[...] = (mine[...].astype(F32) + other[...].astype(F32)).astype(total.dtype)


def sketch_kernel(pairs, scale, info, after, *refs):
    projs = [refs[p * 4 : (p + 1) * 4] for p in range(pairs)]
    acts, out, token = refs[pairs * 4 :]
    slots, rows, both = projs[0][0].shape
    rank = both // 2
    chunk = out.shape[1] // 2
    live = live_slots(info)

    def one(ref, i):
        lower = left_lanes((rank // 2, both), rank)
        for k in range(slots):

            @pl.when(k < live)
            def _():
                full = mm(ref[k], acts[k, i], TN)
                for m in range(chunk):
                    even = full[: rank // 2, m * both : (m + 1) * both]
                    uneven = full[rank // 2 : rank, m * both : (m + 1) * both]
                    out[k, i * chunk + m] = (jnp.where(lower, even, uneven) * scale).astype(BF16)

            @pl.when(k >= live)
            def _():
                out[k, i * chunk : (i + 1) * chunk] = jnp.zeros((chunk, rank // 2, both), BF16)

    for p in range(pairs):
        active, odd = here(pairs - 1 - p)

        @pl.when(jnp.logical_and(active, odd))
        def _():
            for i in range(2):
                one(projs[p][i], i)

        @pl.when(jnp.logical_and(active, jnp.logical_not(odd)))
        def _():
            for i in range(2):
                one(projs[p][2 + i], i)


def collect_kernel(pairs, after, *refs):
    out, token = refs[-2:]
    count = (len(refs) - 2) // (2 * pairs)
    chunk = refs[0].shape[0]
    for p in range(pairs):
        active, odd = here(pairs - 1 - p)
        for parity in (1, 0):

            @pl.when(jnp.logical_and(active, odd if parity else jnp.logical_not(odd)))
            def _():
                for c in range(count):
                    out[c * chunk : (c + 1) * chunk] = refs[(2 * p + 1 - parity) * count + c][...]


def last_kernel(after, *refs):
    out = refs[-1]
    groups = [(refs[i], refs[i + 1]) for i in range(0, len(refs) - 1, 2)]
    slots, micro, parts, lanes = groups[0][0].shape
    for k in range(slots):
        total = jnp.concatenate([mine[k].astype(F32) + other[k].astype(F32) for mine, other in groups])
        total = jnp.swapaxes(total, 0, 1)
        for i in range(parts):
            out[k, :, i * lanes : (i + 1) * lanes] = total[i]


def swaps(axes):
    for axis in axes:
        peers = lax.axis_size(axis)
        if peers & (peers - 1):
            yield axis, 0
        else:
            by = 1
            while by < peers:
                yield axis, by
                by *= 2


def exchange(x, axis, by):
    if not by:
        return lax.psum(x.astype(F32), axis).astype(BF16) - x
    return lax.ppermute(x, axis, [(i, i ^ by) for i in range(lax.axis_size(axis))])


def shards(grad_out, activations, mixing, proj_tiles, proj_blocks, section_sizes):
    sections = lax.axis_size("pipe")
    section = lax.axis_index("pipe")
    micro, tokens, width = grad_out.shape
    slots = activations.shape[1]
    heads, head_size = mixing.shape[2:4]
    both = proj_tiles.shape[4]
    rank = both // 2
    scale = 1.0 / math.sqrt(tokens * lax.axis_size("dp"))
    pairs = sections // 2
    count = 4
    chunk = micro // count
    rows = chunk * tokens
    top_pair = pairs - 1
    last = None
    weights = iter(WORK)

    def call(kernel, name, ins, specs, outs, scratch=(), work=LIGHT, alias={}):
        outs = tuple(jax.ShapeDtypeStruct(s, t) for s, t in outs)
        return pl.pallas_call(
            kernel,
            out_shape=outs,
            in_specs=specs,
            out_specs=(VMEM,) * len(outs),
            scratch_shapes=scratch,
            input_output_aliases=alias,
            compiler_params=PARAMS,
            cost_estimate=pl.CostEstimate(flops=work, bytes_accessed=1000, transcendentals=0),
            name=name,
        )(*ins)

    def in_turn(kernel, name, first, ins, outs, more=(), scratch=(), work=LIGHT, alias=None):
        nonlocal last
        work = 10**6 * next(weights, 1)
        ins = [*first, last, *ins]
        res = call(kernel, name, ins, [VMEM] * len(ins), [*outs, (FLAG, F32), *more], scratch, work, alias or {})
        last = res[len(outs)]
        return [*res[: len(outs)], *res[len(outs) + 1 :]]

    step_outs = [((chunk, tokens, width), BF16), ((slots, rows, both), BF16)]
    slope_out = ((slots, chunk, tokens, width), F32)
    part_out = ((slots, rows, both), BF16)
    grad, proj, slope, part, next_slope, next_part, acts, top, mix_act, mix_grad, info = call(
        functools.partial(first_kernel, top_pair),
        "first",
        [
            pltpu.with_memory_space_constraint(x, pltpu.HBM)
            for x in (section_sizes, proj_blocks.transpose(1, 0, 2), grad_out, activations[0], mixing[0], proj_tiles[0])
        ],
        [HBM] * 6,
        [
            *step_outs,
            slope_out,
            part_out,
            slope_out,
            part_out,
            (activations.shape[1:], BF16),
            (grad_out.shape, BF16),
            ((slots, heads, head_size, head_size + both), BF16),
            ((slots, heads, head_size + both, head_size), BF16),
            (FLAG, F32),
        ],
        [
            pltpu.SMEM(section_sizes.shape, jnp.int32),
            pltpu.SMEM((slots, 1, proj_blocks.shape[2]), jnp.int32),
            pltpu.VMEM(proj_tiles.shape[1:], BF16),
            pltpu.SemaphoreType.DMA((6 * slots + 4,)),
        ],
    )
    last = info
    slopes = [slope, next_slope]
    swap = [(i, i ^ 1) for i in range(sections)]
    grads = [([], []) for _ in range(pairs)]
    projs = [([], []) for _ in range(pairs)]
    hops = [[] for _ in range(pairs)]
    core = [[] for _ in range(pairs)]

    def keep(p, odd, even, grad, proj):
        for parity, there in ((0, even), (1, odd)):
            if there:
                grads[p][parity].append(grad)
                projs[p][parity].append(proj)
        if odd:
            core[p].append(lax.ppermute(grad, "pipe", swap))
        if even and p + 1 < pairs:
            source = sections - 2 - 2 * p
            hop = [(source, source - 1)]
            if len(hops[p]) >= count - 2:
                hop = [(i, (i - 1) % sections) for i in range(sections)]
            hops[p].append(lax.ppermute(grad, "pipe", hop))

    def top_step(at):
        ins, scratch = [core[0][at - 1], slopes[at - 1]], []
        if at < count:
            ins += [top, acts, mix_act]
            scratch.append(pltpu.VMEM(slope_out[0], F32))
        kernel = functools.partial(top_kernel, top_pair, at, at < count)
        keep(0, at < count, True, *in_turn(kernel, "top", [info, mix_grad], ins, step_outs, scratch=scratch))

    def step(p, parity, at):
        source = hops[p - 1][at] if parity else core[p][at]
        kernel = functools.partial(step_kernel, top_pair - p, parity)
        keep(p, parity, not parity, *in_turn(kernel, "step", [info, mix_grad], [source, slopes[at]], step_outs))

    class Sum:
        def __init__(self, value, turns):
            self.mine, self.turns = value, turns
            self.go()

        def go(self):
            self.other = exchange(self.mine, *self.turns.pop(0))

        def turn(self, work=LIGHT):
            self.mine = in_turn(add_kernel, "add", [self.mine, self.other], [], [(self.mine.shape, BF16)], work=work)[0]
            self.go()

    def collect():
        ins = [grad for pair in grads for parity in (1, 0) for grad in pair[parity]]
        return in_turn(functools.partial(collect_kernel, pairs), "collect", [], ins, [(grad_out.shape, BF16)])[0]

    def sketch(group):
        out = ((slots, 2, rows, chunk * both), BF16)
        kernel = functools.partial(widen_kernel, group, chunk)
        wide = in_turn(kernel, "widen", [act_sum.mine, act_sum.other], [], [out])[0]
        ins = []
        for p in range(pairs):
            for parity in (1, 0):
                ins += projs[p][parity][2 * group : 2 * group + 2]
        kernel = functools.partial(sketch_kernel, pairs, scale)
        out = ((slots, 2 * chunk, rank // 2, both), BF16)
        return in_turn(kernel, "sketch", [info], [*ins, wide], [out])[0]

    low = pairs - 1
    act_turns = list(swaps(("tensor",)))
    turns = list(swaps(("dp", "tensor")))
    keep(0, True, False, grad, proj)
    slope, act_part = in_turn(
        functools.partial(beside_kernel, top_pair),
        "beside",
        [info, acts, mix_act],
        [part, next_part],
        [slope_out, ((2, *part_out[0]), BF16)],
        scratch=[pltpu.VMEM(*part_out)],
    )
    slopes.append(slope)
    act_sum = Sum(act_part, act_turns)
    top_step(1)
    top_step(2)
    kernel = functools.partial(slope_kernel, top_pair, 3 * chunk)
    slopes += in_turn(kernel, "slope", [info, acts, mix_act], [], [slope_out])
    while act_sum.turns:
        act_sum.turn()
    top_step(3)
    for p in range(1, pairs):
        step(p, 1, 0)
        if p == 1:
            top_step(count)
        else:
            step(p - 1, 0, 3)
        step(p, 1, 1)
        step(p, 0, 0)
        step(p, 0, 1)
        if p < low:
            step(p, 1, 2)
            step(p, 1, 3)
            step(p, 0, 2)
    early = Sum(sketch(0), list(swaps(("tensor", "dp"))))
    step(low, 1, 2)
    step(low, 1, 3)
    step(low, 0, 2)
    step(low, 0, 3)
    late = Sum(sketch(1), list(turns))
    segment_out = None
    while late.turns:
        if early.turns:
            early.turn()
        late.turn()
        if segment_out is None:
            segment_out = collect()
    ins = [last, early.mine, early.other, late.mine, late.other]
    (total,) = call(last_kernel, "last", ins, [VMEM] * 5, [((slots, micro, rank * rank), F32)])

    return (segment_out[None], total[None])


def solution(mesh):
    return jax.shard_map(
        shards,
        mesh=mesh,
        in_specs=(
            P(None, "dp", "tensor"),
            P("pipe", None, None, "dp", "tensor"),
            P("pipe", None, "tensor", None, None),
            P("pipe", None, None, None, None),
            P("pipe", None, None),
            P(),
        ),
        out_specs=(P("pipe", None, "dp", "tensor"), P("pipe", None, None, None)),
        check_vma=False,
    )
```

```python
import functools
import math

import jax
import jax.numpy as jnp
from jax import lax
from jax.experimental import pallas as pl
from jax.experimental.pallas import tpu as pltpu
from jax.sharding import PartitionSpec as P

F32 = jnp.float32
BF16 = jnp.bfloat16
VMEM = pl.BlockSpec(memory_space=pltpu.VMEM)
HBM = pl.BlockSpec(memory_space=pltpu.HBM)
PARAMS = pltpu.CompilerParams(vmem_limit_bytes=16 * 1024 * 1024)
NN = (((1,), (0,)), ((), ()))
NT = (((1,), (1,)), ((), ()))
TN = (((0,), (0,)), ((), ()))
FLAG = (8, 128)
LIGHT = 1000
WORK = (3000, 1000, 6000, 1000, 10000, 6000, 10000, 6000, 10000, 3000, 1, 10000, 2000, 10000, 300, 6000, 1, 300, 1, 10000, 2000, 10000, 3000, 2000, 3000, 1)


def mm(a, b, dims=NN):
    return lax.dot_general(a, b, dims, preferred_element_type=F32)


def silu_slope(value):
    sig = 0.5 + 0.5 * jnp.tanh(0.5 * value)
    return sig * (1.0 + value * (1.0 - sig))


def left_lanes(shape, rank):
    return lax.broadcasted_iota(jnp.int32, shape, len(shape) - 1) < rank


def head_lanes(h, head_size):
    return slice(h * head_size, (h + 1) * head_size)


def live_slots(info):
    return jnp.max(info[...]).astype(jnp.int32)


def here(pair):
    section = lax.axis_index("pipe")
    return section // 2 == pair, section % 2 == 1


def slopes_of(k, at, acts, mix_act, slopes, part=None):
    chunk, tokens, width = slopes.shape[1:]
    heads, head_size = mix_act.shape[1], mix_act.shape[2]
    rows = chunk * tokens
    total = 0.0
    for h in range(heads):
        act = acts[k, at : at + chunk, :, head_lanes(h, head_size)].reshape(rows, head_size)
        if part is None:
            pre = mm(act, mix_act[k, h, :, :head_size])
        else:
            both = mm(act, mix_act[k, h])
            total += both[:, head_size:]
            pre = both[:, :head_size]
        slope = silu_slope(pre).astype(slopes.dtype)
        slopes[k, :, :, head_lanes(h, head_size)] = slope.reshape(chunk, tokens, head_size)
    if part is not None:
        part[k] = total.astype(BF16)


def project_of(k, at, chunk, acts, mix_act):
    tokens = acts.shape[2]
    heads, head_size = mix_act.shape[1], mix_act.shape[2]
    total = 0.0
    for h in range(heads):
        act = acts[k, at : at + chunk, :, head_lanes(h, head_size)].reshape(chunk * tokens, head_size)
        total += mm(act, mix_act[k, h, :, head_size:])
    return total


def chain(live, source, slopes, mix_grad, grad, proj):
    chunk, tokens, width = grad.shape
    heads, head_size = mix_grad.shape[1], mix_grad.shape[3]
    rows = chunk * tokens
    grad[...] = source

    def slot(i, _):
        k = live - 1 - i
        old, both = [], []
        for h in range(heads):
            lanes = head_lanes(h, head_size)
            g = grad[:, :, lanes].reshape(rows, head_size).astype(F32)
            delta = (g * slopes[k, :, :, lanes].reshape(rows, head_size).astype(F32)).astype(BF16)
            old.append(g)
            both.append(mm(delta, mix_grad[k, h], NT))
        total = jnp.zeros((rows, proj.shape[2]), F32)
        for h in range(heads):
            lanes = head_lanes(h, head_size)
            grad[:, :, lanes] = (old[h] + both[h][:, :head_size]).astype(BF16).reshape(chunk, tokens, head_size)
            total += both[h][:, head_size:]
        proj[k] = total.astype(BF16)
        return 0

    lax.fori_loop(0, live, slot, 0)


def spread_tiles(k, blocks, tiles, mix_act, mix_grad):
    picks, head_size, both = tiles.shape[1:]
    rank = both // 2
    heads = mix_act.shape[1]
    first_head = lax.axis_index("tensor") * heads
    row = lax.broadcasted_iota(jnp.int32, (both, both), 0)
    col = lax.broadcasted_iota(jnp.int32, (both, both), 1)
    twice = (row == col % rank).astype(BF16)
    order = rank + jnp.where(row < rank // 2, 2 * row, 2 * row - rank + 1)
    split = jnp.logical_and(col == order, row < rank).astype(BF16)
    for j in range(picks):
        own = blocks[k, 0, j] - first_head

        @pl.when(jnp.logical_and(own >= 0, own < heads))
        def _():
            tile = tiles[k, j]
            mix_act[k, own, :, head_size:] = mm(tile, twice).astype(BF16)
            mix_grad[k, own, head_size:, :] = mm(split, tile, NT).astype(BF16)


def first_kernel(
    pair, sizes_in, blocks_in, top, acts, mixing, tiles,
    grad, proj, slopes, part, next_slopes, next_part, acts_v, top_v, mix_act, mix_grad, info,
    sizes, blocks, tiles_v, sems,
):
    slots = acts.shape[0]
    head_size = mixing.shape[2]
    chunk, micro = grad.shape[0], acts.shape[1]
    copies = []

    def load(src, dst):
        copy = pltpu.make_async_copy(src, dst, sems.at[len(copies)])
        copy.start()
        copies.append(copy)
        return copy

    order = range(slots - 1, -1, -1)
    scalars = (load(sizes_in, sizes), load(blocks_in, blocks))
    spread = {k: load(tiles.at[k], tiles_v.at[k]) for k in order}
    need = {
        k: (
            load(mixing.at[k], mix_act.at[k, :, :, pl.ds(0, head_size)]),
            load(acts.at[k, pl.ds(0, chunk)], acts_v.at[k, pl.ds(0, chunk)]),
        )
        for k in order
    }
    first = [load(mixing.at[k], mix_grad.at[k, :, pl.ds(0, head_size), :]) for k in order]
    first.append(load(top.at[pl.ds(0, chunk)], top_v.at[pl.ds(0, chunk)]))
    second = [load(acts.at[k, pl.ds(chunk, chunk)], acts_v.at[k, pl.ds(chunk, chunk)]) for k in order]
    left = micro - 2 * chunk
    rest = [load(acts.at[k, pl.ds(2 * chunk, left)], acts_v.at[k, pl.ds(2 * chunk, left)]) for k in order]
    rest.append(load(top.at[pl.ds(chunk, micro - chunk)], top_v.at[pl.ds(chunk, micro - chunk)]))
    for k in order:
        mix_act[k, :, :, head_size:] = jnp.zeros((*mix_act.shape[1:3], mix_act.shape[3] - head_size), BF16)
        mix_grad[k, :, head_size:, :] = jnp.zeros((mix_grad.shape[1], mix_grad.shape[2] - head_size, head_size), BF16)
    for copy in scalars:
        copy.wait()
    live = sizes[lax.axis_index("pipe")]
    info[...] = jnp.full(info.shape, live.astype(F32))
    for k in order:
        spread[k].wait()
        pl.when(k < live)(functools.partial(spread_tiles, k, blocks, tiles_v, mix_act, mix_grad))
    for k in order:
        for copy in need[k]:
            copy.wait()
        pl.when(k < live)(functools.partial(slopes_of, k, 0, acts_v, mix_act, slopes, part))
    for copy in first:
        copy.wait()
    active, odd = here(pair)
    ahead = jnp.logical_and(active, odd)

    @pl.when(ahead)
    def _():
        chain(live, top_v[:chunk], slopes, mix_grad, grad, proj)

    for copy in second:
        copy.wait()
    for k in order:
        pl.when(jnp.logical_and(k < live, jnp.logical_not(ahead)))(
            functools.partial(slopes_of, k, chunk, acts_v, mix_act, next_slopes, next_part)
        )
    for copy in rest:
        copy.wait()


def lay(act_part, group, k, one, two):
    left = left_lanes(one.shape, one.shape[1] // 2)
    act_part[group, k] = jnp.where(left, one, two).astype(BF16)


def beside_kernel(pair, info, acts, mix_act, after, first_part, second_part, slopes, act_part, token, part):
    chunk = slopes.shape[1]
    live = live_slots(info)
    active, odd = here(pair)
    ahead = jnp.logical_and(active, odd)
    for k in range(acts.shape[0]):

        @pl.when(jnp.logical_and(k < live, ahead))
        def _():
            rest = project_of(k, chunk, 3 * chunk, acts, mix_act)
            rows = rest.shape[0] // 3
            lay(act_part, 0, k, first_part[k], rest[:rows])
            lay(act_part, 1, k, rest[rows : 2 * rows], rest[2 * rows :])

        @pl.when(jnp.logical_and(k < live, jnp.logical_not(ahead)))
        def _():
            slopes_of(k, 2 * chunk, acts, mix_act, slopes, part)
            lay(act_part, 0, k, first_part[k], second_part[k])
            lay(act_part, 1, k, part[k], project_of(k, 3 * chunk, chunk, acts, mix_act))


def slope_kernel(pair, at, info, acts, mix_act, after, slopes, token):
    live = live_slots(info)
    active, odd = here(pair)
    ahead = jnp.logical_and(active, odd)
    for k in range(acts.shape[0]):
        pl.when(jnp.logical_and(k < live, jnp.logical_not(ahead)))(
            functools.partial(slopes_of, k, at, acts, mix_act, slopes)
        )


def top_kernel(pair, at, has_odd, info, mix_grad, after, even_in, even_slopes, *refs):
    refs = list(refs)
    top, acts, mix_act = (refs.pop(0), refs.pop(0), refs.pop(0)) if has_odd else (None, None, None)
    grad, proj, token = refs[:3]
    slopes = refs[3] if has_odd else None
    active, odd = here(pair)

    @pl.when(jnp.logical_and(active, jnp.logical_not(odd)))
    def _():
        chain(live_slots(info), even_in[...], even_slopes, mix_grad, grad, proj)

    if has_odd:
        chunk = grad.shape[0]

        @pl.when(jnp.logical_and(active, odd))
        def _():
            live = live_slots(info)
            for k in range(acts.shape[0] - 1, -1, -1):
                pl.when(k < live)(functools.partial(slopes_of, k, at * chunk, acts, mix_act, slopes))
            chain(live, top[at * chunk : (at + 1) * chunk], slopes, mix_grad, grad, proj)


def step_kernel(pair, parity, info, mix_grad, after, source, slopes, grad, proj, token):
    active, odd = here(pair)

    @pl.when(jnp.logical_and(active, odd if parity else jnp.logical_not(odd)))
    def _():
        chain(live_slots(info), source[...], slopes, mix_grad, grad, proj)


def widen_kernel(group, chunk, mine, other, after, out, token):
    slots, rows, both = mine.shape[1:]
    rank = both // 2
    batch = lax.broadcasted_iota(jnp.int32, (rows, both), 0) // (rows // chunk)
    left = left_lanes((rows, both), rank)
    for k in range(slots):
        act = mine[group, k].astype(F32) + other[group, k].astype(F32)
        swapped = pltpu.roll(act, rank, 1)
        for i in range(2):
            one = jnp.where(left, swapped, act) if i else jnp.where(left, act, swapped)
            for m in range(chunk):
                out[k, i, :, m * both : (m + 1) * both] = jnp.where(batch == m, one, 0.0).astype(BF16)


def add_kernel(mine, other, after, total, token):
    total[...] = (mine[...].astype(F32) + other[...].astype(F32)).astype(total.dtype)


def sketch_kernel(pairs, scale, info, after, *refs):
    projs = [refs[p * 4 : (p + 1) * 4] for p in range(pairs)]
    acts, out, token = refs[pairs * 4 :]
    slots, rows, both = projs[0][0].shape
    rank = both // 2
    chunk = out.shape[1] // 2
    live = live_slots(info)

    def one(ref, i):
        lower = left_lanes((rank // 2, both), rank)
        for k in range(slots):

            @pl.when(k < live)
            def _():
                full = mm(ref[k], acts[k, i], TN)
                for m in range(chunk):
                    even = full[: rank // 2, m * both : (m + 1) * both]
                    uneven = full[rank // 2 : rank, m * both : (m + 1) * both]
                    out[k, i * chunk + m] = (jnp.where(lower, even, uneven) * scale).astype(BF16)

            @pl.when(k >= live)
            def _():
                out[k, i * chunk : (i + 1) * chunk] = jnp.zeros((chunk, rank // 2, both), BF16)

    for p in range(pairs):
        active, odd = here(pairs - 1 - p)

        @pl.when(jnp.logical_and(active, odd))
        def _():
            for i in range(2):
                one(projs[p][i], i)

        @pl.when(jnp.logical_and(active, jnp.logical_not(odd)))
        def _():
            for i in range(2):
                one(projs[p][2 + i], i)


def collect_kernel(pairs, after, *refs):
    out, token = refs[-2:]
    count = (len(refs) - 2) // (2 * pairs)
    chunk = refs[0].shape[0]
    for p in range(pairs):
        active, odd = here(pairs - 1 - p)
        for parity in (1, 0):

            @pl.when(jnp.logical_and(active, odd if parity else jnp.logical_not(odd)))
            def _():
                for c in range(count):
                    out[c * chunk : (c + 1) * chunk] = refs[(2 * p + 1 - parity) * count + c][...]


def last_kernel(after, *refs):
    out = refs[-1]
    groups = [(refs[i], refs[i + 1]) for i in range(0, len(refs) - 1, 2)]
    slots, micro, parts, lanes = groups[0][0].shape
    for k in range(slots):
        total = jnp.concatenate([mine[k].astype(F32) + other[k].astype(F32) for mine, other in groups])
        total = jnp.swapaxes(total, 0, 1)
        for i in range(parts):
            out[k, :, i * lanes : (i + 1) * lanes] = total[i]


def swaps(axes):
    for axis in axes:
        peers = lax.axis_size(axis)
        if peers & (peers - 1):
            yield axis, 0
        else:
            by = 1
            while by < peers:
                yield axis, by
                by *= 2


def exchange(x, axis, by):
    if not by:
        return lax.psum(x.astype(F32), axis).astype(BF16) - x
    return lax.ppermute(x, axis, [(i, i ^ by) for i in range(lax.axis_size(axis))])


def shards(grad_out, activations, mixing, proj_tiles, proj_blocks, section_sizes):
    sections = lax.axis_size("pipe")
    section = lax.axis_index("pipe")
    micro, tokens, width = grad_out.shape
    slots = activations.shape[1]
    heads, head_size = mixing.shape[2:4]
    both = proj_tiles.shape[4]
    rank = both // 2
    scale = 1.0 / math.sqrt(tokens * lax.axis_size("dp"))
    pairs = sections // 2
    count = 4
    chunk = micro // count
    rows = chunk * tokens
    top_pair = pairs - 1
    last = None
    weights = iter(WORK)

    def call(kernel, name, ins, specs, outs, scratch=(), work=LIGHT, alias={}):
        outs = tuple(jax.ShapeDtypeStruct(s, t) for s, t in outs)
        return pl.pallas_call(
            kernel,
            out_shape=outs,
            in_specs=specs,
            out_specs=(VMEM,) * len(outs),
            scratch_shapes=scratch,
            input_output_aliases=alias,
            compiler_params=PARAMS,
            cost_estimate=pl.CostEstimate(flops=work, bytes_accessed=1000, transcendentals=0),
            name=name,
        )(*ins)

    def in_turn(kernel, name, first, ins, outs, more=(), scratch=(), work=LIGHT, alias=None):
        nonlocal last
        work = 10**6 * next(weights, 1)
        ins = [*first, last, *ins]
        res = call(kernel, name, ins, [VMEM] * len(ins), [*outs, (FLAG, F32), *more], scratch, work, alias or {})
        last = res[len(outs)]
        return [*res[: len(outs)], *res[len(outs) + 1 :]]

    step_outs = [((chunk, tokens, width), BF16), ((slots, rows, both), BF16)]
    slope_out = ((slots, chunk, tokens, width), F32)
    part_out = ((slots, rows, both), BF16)
    grad, proj, slope, part, next_slope, next_part, acts, top, mix_act, mix_grad, info = call(
        functools.partial(first_kernel, top_pair),
        "first",
        [
            pltpu.with_memory_space_constraint(x, pltpu.HBM)
            for x in (section_sizes, proj_blocks.transpose(1, 0, 2), grad_out, activations[0], mixing[0], proj_tiles[0])
        ],
        [HBM] * 6,
        [
            *step_outs,
            slope_out,
            part_out,
            slope_out,
            part_out,
            (activations.shape[1:], BF16),
            (grad_out.shape, BF16),
            ((slots, heads, head_size, head_size + both), BF16),
            ((slots, heads, head_size + both, head_size), BF16),
            (FLAG, F32),
        ],
        [
            pltpu.SMEM(section_sizes.shape, jnp.int32),
            pltpu.SMEM((slots, 1, proj_blocks.shape[2]), jnp.int32),
            pltpu.VMEM(proj_tiles.shape[1:], BF16),
            pltpu.SemaphoreType.DMA((6 * slots + 4,)),
        ],
    )
    last = info
    slopes = [slope, next_slope]
    swap = [(i, i ^ 1) for i in range(sections)]
    grads = [([], []) for _ in range(pairs)]
    projs = [([], []) for _ in range(pairs)]
    hops = [[] for _ in range(pairs)]
    core = [[] for _ in range(pairs)]

    def keep(p, odd, even, grad, proj):
        for parity, there in ((0, even), (1, odd)):
            if there:
                grads[p][parity].append(grad)
                projs[p][parity].append(proj)
        if odd:
            core[p].append(lax.ppermute(grad, "pipe", swap))
        if even and p + 1 < pairs:
            source = sections - 2 - 2 * p
            hop = [(source, source - 1)]
            if len(hops[p]) >= count - 2:
                hop = [(i, (i - 1) % sections) for i in range(sections)]
            hops[p].append(lax.ppermute(grad, "pipe", hop))

    def top_step(at):
        ins, scratch = [core[0][at - 1], slopes[at - 1]], []
        if at < count:
            ins += [top, acts, mix_act]
            scratch.append(pltpu.VMEM(slope_out[0], F32))
        kernel = functools.partial(top_kernel, top_pair, at, at < count)
        keep(0, at < count, True, *in_turn(kernel, "top", [info, mix_grad], ins, step_outs, scratch=scratch))

    def step(p, parity, at):
        source = hops[p - 1][at] if parity else core[p][at]
        kernel = functools.partial(step_kernel, top_pair - p, parity)
        keep(p, parity, not parity, *in_turn(kernel, "step", [info, mix_grad], [source, slopes[at]], step_outs))

    class Sum:
        def __init__(self, value, turns):
            self.mine, self.turns = value, turns
            self.go()

        def go(self):
            self.other = exchange(self.mine, *self.turns.pop(0))

        def turn(self, work=LIGHT):
            self.mine = in_turn(add_kernel, "add", [self.mine, self.other], [], [(self.mine.shape, BF16)], work=work)[0]
            self.go()

    def collect():
        ins = [grad for pair in grads for parity in (1, 0) for grad in pair[parity]]
        return in_turn(functools.partial(collect_kernel, pairs), "collect", [], ins, [(grad_out.shape, BF16)])[0]

    def sketch(group):
        out = ((slots, 2, rows, chunk * both), BF16)
        kernel = functools.partial(widen_kernel, group, chunk)
        wide = in_turn(kernel, "widen", [act_sum.mine, act_sum.other], [], [out])[0]
        ins = []
        for p in range(pairs):
            for parity in (1, 0):
                ins += projs[p][parity][2 * group : 2 * group + 2]
        kernel = functools.partial(sketch_kernel, pairs, scale)
        out = ((slots, 2 * chunk, rank // 2, both), BF16)
        return in_turn(kernel, "sketch", [info], [*ins, wide], [out])[0]

    low = pairs - 1
    act_turns = list(swaps(("tensor",)))
    turns = list(swaps(("dp", "tensor")))
    keep(0, True, False, grad, proj)
    slope, act_part = in_turn(
        functools.partial(beside_kernel, top_pair),
        "beside",
        [info, acts, mix_act],
        [part, next_part],
        [slope_out, ((2, *part_out[0]), BF16)],
        scratch=[pltpu.VMEM(*part_out)],
    )
    slopes.append(slope)
    act_sum = Sum(act_part, act_turns)
    top_step(1)
    top_step(2)
    kernel = functools.partial(slope_kernel, top_pair, 3 * chunk)
    slopes += in_turn(kernel, "slope", [info, acts, mix_act], [], [slope_out])
    while act_sum.turns:
        act_sum.turn()
    top_step(3)
    for p in range(1, pairs):
        step(p, 1, 0)
        if p == 1:
            top_step(count)
        else:
            step(p - 1, 0, 3)
        step(p, 1, 1)
        step(p, 0, 0)
        step(p, 0, 1)
        if p < low:
            step(p, 1, 2)
            step(p, 1, 3)
            step(p, 0, 2)
    early = Sum(sketch(0), list(swaps(("tensor", "dp"))))
    step(low, 1, 2)
    step(low, 1, 3)
    step(low, 0, 2)
    step(low, 0, 3)
    late = Sum(sketch(1), list(turns))
    segment_out = None
    while late.turns:
        if early.turns:
            early.turn()
        late.turn()
        if segment_out is None:
            segment_out = collect()
    ins = [last, early.mine, early.other, late.mine, late.other]
    (total,) = call(last_kernel, "last", ins, [VMEM] * 5, [((slots, micro, rank * rank), F32)])

    return (segment_out[None], total[None])


def solution(mesh):
    return jax.shard_map(
        shards,
        mesh=mesh,
        in_specs=(
            P(None, "dp", "tensor"),
            P("pipe", None, None, "dp", "tensor"),
            P("pipe", None, "tensor", None, None),
            P("pipe", None, None, None, None),
            P("pipe", None, None),
            P(),
        ),
        out_specs=(P("pipe", None, "dp", "tensor"), P("pipe", None, None, None)),
        check_vma=False,
    )
```

```python
import functools
import math

import jax
import jax.numpy as jnp
from jax import lax
from jax.experimental import pallas as pl
from jax.experimental.pallas import tpu as pltpu
from jax.sharding import PartitionSpec as P

F32 = jnp.float32
BF16 = jnp.bfloat16
VMEM = pl.BlockSpec(memory_space=pltpu.VMEM)
HBM = pl.BlockSpec(memory_space=pltpu.HBM)
PARAMS = pltpu.CompilerParams(vmem_limit_bytes=16 * 1024 * 1024)
NN = (((1,), (0,)), ((), ()))
NT = (((1,), (1,)), ((), ()))
TN = (((0,), (0,)), ((), ()))
FLAG = (8, 128)
LIGHT = 1000
WORK = (3000, 1000, 6000, 1000, 10000, 6000, 10000, 6000, 10000, 3000, 1, 10000, 2000, 10000, 300, 6000, 1, 300, 1, 10000, 2000, 10000, 3000, 2000, 3000, 1)


def mm(a, b, dims=NN):
    return lax.dot_general(a, b, dims, preferred_element_type=F32)


def silu_slope(value):
    sig = 0.5 + 0.5 * jnp.tanh(0.5 * value)
    return sig * (1.0 + value * (1.0 - sig))


def left_lanes(shape, rank):
    return lax.broadcasted_iota(jnp.int32, shape, len(shape) - 1) < rank


def head_lanes(h, head_size):
    return slice(h * head_size, (h + 1) * head_size)


def live_slots(info):
    return jnp.max(info[...]).astype(jnp.int32)


def here(pair):
    section = lax.axis_index("pipe")
    return section // 2 == pair, section % 2 == 1


def slopes_of(k, at, acts, mix_act, slopes, part=None):
    chunk, tokens, width = slopes.shape[1:]
    heads, head_size = mix_act.shape[1], mix_act.shape[2]
    rows = chunk * tokens
    total = 0.0
    for h in range(heads):
        act = acts[k, at : at + chunk, :, head_lanes(h, head_size)].reshape(rows, head_size)
        if part is None:
            pre = mm(act, mix_act[k, h, :, :head_size])
        else:
            both = mm(act, mix_act[k, h])
            total += both[:, head_size:]
            pre = both[:, :head_size]
        slope = silu_slope(pre).astype(slopes.dtype)
        slopes[k, :, :, head_lanes(h, head_size)] = slope.reshape(chunk, tokens, head_size)
    if part is not None:
        part[k] = total.astype(BF16)


def project_of(k, at, chunk, acts, mix_act):
    tokens = acts.shape[2]
    heads, head_size = mix_act.shape[1], mix_act.shape[2]
    total = 0.0
    for h in range(heads):
        act = acts[k, at : at + chunk, :, head_lanes(h, head_size)].reshape(chunk * tokens, head_size)
        total += mm(act, mix_act[k, h, :, head_size:])
    return total


def chain(live, source, slopes, mix_grad, grad, proj):
    chunk, tokens, width = grad.shape
    heads, head_size = mix_grad.shape[1], mix_grad.shape[3]
    rows = chunk * tokens
    grad[...] = source

    def slot(i, _):
        k = live - 1 - i
        old, both = [], []
        for h in range(heads):
            lanes = head_lanes(h, head_size)
            g = grad[:, :, lanes].reshape(rows, head_size).astype(F32)
            delta = (g * slopes[k, :, :, lanes].reshape(rows, head_size).astype(F32)).astype(BF16)
            old.append(g)
            both.append(mm(delta, mix_grad[k, h], NT))
        total = jnp.zeros((rows, proj.shape[2]), F32)
        for h in range(heads):
            lanes = head_lanes(h, head_size)
            grad[:, :, lanes] = (old[h] + both[h][:, :head_size]).astype(BF16).reshape(chunk, tokens, head_size)
            total += both[h][:, head_size:]
        proj[k] = total.astype(BF16)
        return 0

    lax.fori_loop(0, live, slot, 0)


def spread_tiles(k, blocks, tiles, mix_act, mix_grad):
    picks, head_size, both = tiles.shape[1:]
    rank = both // 2
    heads = mix_act.shape[1]
    first_head = lax.axis_index("tensor") * heads
    row = lax.broadcasted_iota(jnp.int32, (both, both), 0)
    col = lax.broadcasted_iota(jnp.int32, (both, both), 1)
    twice = (row == col % rank).astype(BF16)
    order = rank + jnp.where(row < rank // 2, 2 * row, 2 * row - rank + 1)
    split = jnp.logical_and(col == order, row < rank).astype(BF16)
    mix_act[k, :, :, head_size:] = jnp.zeros((heads, head_size, both), BF16)
    mix_grad[k, :, head_size:, :] = jnp.zeros((heads, both, head_size), BF16)
    for j in range(picks):
        own = blocks[k, 0, j] - first_head

        @pl.when(jnp.logical_and(own >= 0, own < heads))
        def _():
            tile = tiles[k, j]
            mix_act[k, own, :, head_size:] = mm(tile, twice).astype(BF16)
            mix_grad[k, own, head_size:, :] = mm(split, tile, NT).astype(BF16)


def first_kernel(
    pair, sizes_in, blocks_in, top, acts, mixing, tiles,
    grad, proj, slopes, part, next_slopes, next_part, acts_v, top_v, mix_act, mix_grad, info,
    sizes, blocks, tiles_v, sems,
):
    slots = acts.shape[0]
    head_size = mixing.shape[2]
    chunk, micro = grad.shape[0], acts.shape[1]
    copies = []

    def load(src, dst):
        copy = pltpu.make_async_copy(src, dst, sems.at[len(copies)])
        copy.start()
        copies.append(copy)
        return copy

    order = range(slots - 1, -1, -1)
    scalars = (load(sizes_in, sizes), load(blocks_in, blocks))
    spread = {k: load(tiles.at[k], tiles_v.at[k]) for k in order}
    need = {
        k: (
            load(mixing.at[k], mix_act.at[k, :, :, pl.ds(0, head_size)]),
            load(acts.at[k, pl.ds(0, chunk)], acts_v.at[k, pl.ds(0, chunk)]),
        )
        for k in order
    }
    first = [load(mixing.at[k], mix_grad.at[k, :, pl.ds(0, head_size), :]) for k in order]
    first.append(load(top.at[pl.ds(0, chunk)], top_v.at[pl.ds(0, chunk)]))
    second = [load(acts.at[k, pl.ds(chunk, chunk)], acts_v.at[k, pl.ds(chunk, chunk)]) for k in order]
    left = micro - 2 * chunk
    rest = [load(acts.at[k, pl.ds(2 * chunk, left)], acts_v.at[k, pl.ds(2 * chunk, left)]) for k in order]
    rest.append(load(top.at[pl.ds(chunk, micro - chunk)], top_v.at[pl.ds(chunk, micro - chunk)]))
    for copy in scalars:
        copy.wait()
    live = sizes[lax.axis_index("pipe")]
    info[...] = jnp.full(info.shape, live.astype(F32))
    for k in order:
        spread[k].wait()
        pl.when(k < live)(functools.partial(spread_tiles, k, blocks, tiles_v, mix_act, mix_grad))
    for k in order:
        for copy in need[k]:
            copy.wait()
        pl.when(k < live)(functools.partial(slopes_of, k, 0, acts_v, mix_act, slopes, part))
    for copy in first + second:
        copy.wait()
    active, odd = here(pair)
    ahead = jnp.logical_and(active, odd)

    @pl.when(ahead)
    def _():
        chain(live, top_v[:chunk], slopes, mix_grad, grad, proj)

    for k in order:
        pl.when(jnp.logical_and(k < live, jnp.logical_not(ahead)))(
            functools.partial(slopes_of, k, chunk, acts_v, mix_act, next_slopes, next_part)
        )
    for copy in rest:
        copy.wait()


def lay(act_part, group, k, one, two):
    left = left_lanes(one.shape, one.shape[1] // 2)
    act_part[group, k] = jnp.where(left, one, two).astype(BF16)


def beside_kernel(pair, info, acts, mix_act, after, first_part, second_part, slopes, act_part, token, part):
    chunk = slopes.shape[1]
    live = live_slots(info)
    active, odd = here(pair)
    ahead = jnp.logical_and(active, odd)
    for k in range(acts.shape[0]):

        @pl.when(jnp.logical_and(k < live, ahead))
        def _():
            rest = project_of(k, chunk, 3 * chunk, acts, mix_act)
            rows = rest.shape[0] // 3
            lay(act_part, 0, k, first_part[k], rest[:rows])
            lay(act_part, 1, k, rest[rows : 2 * rows], rest[2 * rows :])

        @pl.when(jnp.logical_and(k < live, jnp.logical_not(ahead)))
        def _():
            slopes_of(k, 2 * chunk, acts, mix_act, slopes, part)
            lay(act_part, 0, k, first_part[k], second_part[k])
            lay(act_part, 1, k, part[k], project_of(k, 3 * chunk, chunk, acts, mix_act))


def slope_kernel(pair, at, info, acts, mix_act, after, slopes, token):
    live = live_slots(info)
    active, odd = here(pair)
    ahead = jnp.logical_and(active, odd)
    for k in range(acts.shape[0]):
        pl.when(jnp.logical_and(k < live, jnp.logical_not(ahead)))(
            functools.partial(slopes_of, k, at, acts, mix_act, slopes)
        )


def top_kernel(pair, at, has_odd, info, mix_grad, after, even_in, even_slopes, *refs):
    refs = list(refs)
    top, acts, mix_act = (refs.pop(0), refs.pop(0), refs.pop(0)) if has_odd else (None, None, None)
    grad, proj, token = refs[:3]
    slopes = refs[3] if has_odd else None
    active, odd = here(pair)

    @pl.when(jnp.logical_and(active, jnp.logical_not(odd)))
    def _():
        chain(live_slots(info), even_in[...], even_slopes, mix_grad, grad, proj)

    if has_odd:
        chunk = grad.shape[0]

        @pl.when(jnp.logical_and(active, odd))
        def _():
            live = live_slots(info)
            for k in range(acts.shape[0] - 1, -1, -1):
                pl.when(k < live)(functools.partial(slopes_of, k, at * chunk, acts, mix_act, slopes))
            chain(live, top[at * chunk : (at + 1) * chunk], slopes, mix_grad, grad, proj)


def step_kernel(pair, parity, info, mix_grad, after, source, slopes, grad, proj, token):
    active, odd = here(pair)

    @pl.when(jnp.logical_and(active, odd if parity else jnp.logical_not(odd)))
    def _():
        chain(live_slots(info), source[...], slopes, mix_grad, grad, proj)


def widen_kernel(group, chunk, mine, other, after, out, token):
    slots, rows, both = mine.shape[1:]
    rank = both // 2
    batch = lax.broadcasted_iota(jnp.int32, (rows, both), 0) // (rows // chunk)
    left = left_lanes((rows, both), rank)
    for k in range(slots):
        act = mine[group, k].astype(F32) + other[group, k].astype(F32)
        swapped = pltpu.roll(act, rank, 1)
        for i in range(2):
            one = jnp.where(left, swapped, act) if i else jnp.where(left, act, swapped)
            for m in range(chunk):
                out[k, i, :, m * both : (m + 1) * both] = jnp.where(batch == m, one, 0.0).astype(BF16)


def add_kernel(mine, other, after, total, token):
    total[...] = (mine[...].astype(F32) + other[...].astype(F32)).astype(total.dtype)


def sketch_kernel(pairs, scale, info, after, *refs):
    projs = [refs[p * 4 : (p + 1) * 4] for p in range(pairs)]
    acts, out, token = refs[pairs * 4 :]
    slots, rows, both = projs[0][0].shape
    rank = both // 2
    chunk = out.shape[1] // 2
    live = live_slots(info)

    def one(ref, i):
        lower = left_lanes((rank // 2, both), rank)
        for k in range(slots):

            @pl.when(k < live)
            def _():
                full = mm(ref[k], acts[k, i], TN)
                for m in range(chunk):
                    even = full[: rank // 2, m * both : (m + 1) * both]
                    uneven = full[rank // 2 : rank, m * both : (m + 1) * both]
                    out[k, i * chunk + m] = (jnp.where(lower, even, uneven) * scale).astype(BF16)

            @pl.when(k >= live)
            def _():
                out[k, i * chunk : (i + 1) * chunk] = jnp.zeros((chunk, rank // 2, both), BF16)

    for p in range(pairs):
        active, odd = here(pairs - 1 - p)

        @pl.when(jnp.logical_and(active, odd))
        def _():
            for i in range(2):
                one(projs[p][i], i)

        @pl.when(jnp.logical_and(active, jnp.logical_not(odd)))
        def _():
            for i in range(2):
                one(projs[p][2 + i], i)


def collect_kernel(pairs, after, *refs):
    out, token = refs[-2:]
    count = (len(refs) - 2) // (2 * pairs)
    chunk = refs[0].shape[0]
    for p in range(pairs):
        active, odd = here(pairs - 1 - p)
        for parity in (1, 0):

            @pl.when(jnp.logical_and(active, odd if parity else jnp.logical_not(odd)))
            def _():
                for c in range(count):
                    out[c * chunk : (c + 1) * chunk] = refs[(2 * p + 1 - parity) * count + c][...]


def rows_kernel(mine, other, after, out, token):
    slots, micro, parts, lanes = mine.shape
    for k in range(slots):
        total = jnp.swapaxes(mine[k].astype(F32) + other[k].astype(F32), 0, 1)
        for i in range(parts):
            out[k, :, i * lanes : (i + 1) * lanes] = total[i]


def last_kernel(after, rows, mine, other, out):
    slots, micro, parts, lanes = mine.shape
    done = rows.shape[1]
    out[:, :done] = rows[...]
    for k in range(slots):
        total = jnp.swapaxes(mine[k].astype(F32) + other[k].astype(F32), 0, 1)
        for i in range(parts):
            out[k, done : done + micro, i * lanes : (i + 1) * lanes] = total[i]


def swaps(axes):
    for axis in axes:
        peers = lax.axis_size(axis)
        if peers & (peers - 1):
            yield axis, 0
        else:
            by = 1
            while by < peers:
                yield axis, by
                by *= 2


def exchange(x, axis, by):
    if not by:
        return lax.psum(x.astype(F32), axis).astype(BF16) - x
    return lax.ppermute(x, axis, [(i, i ^ by) for i in range(lax.axis_size(axis))])


def shards(grad_out, activations, mixing, proj_tiles, proj_blocks, section_sizes):
    sections = lax.axis_size("pipe")
    section = lax.axis_index("pipe")
    micro, tokens, width = grad_out.shape
    slots = activations.shape[1]
    heads, head_size = mixing.shape[2:4]
    both = proj_tiles.shape[4]
    rank = both // 2
    scale = 1.0 / math.sqrt(tokens * lax.axis_size("dp"))
    pairs = sections // 2
    count = 4
    chunk = micro // count
    rows = chunk * tokens
    top_pair = pairs - 1
    last = None
    weights = iter(WORK)

    def call(kernel, name, ins, specs, outs, scratch=(), work=LIGHT, alias={}):
        outs = tuple(jax.ShapeDtypeStruct(s, t) for s, t in outs)
        return pl.pallas_call(
            kernel,
            out_shape=outs,
            in_specs=specs,
            out_specs=(VMEM,) * len(outs),
            scratch_shapes=scratch,
            input_output_aliases=alias,
            compiler_params=PARAMS,
            cost_estimate=pl.CostEstimate(flops=work, bytes_accessed=1000, transcendentals=0),
            name=name,
        )(*ins)

    def in_turn(kernel, name, first, ins, outs, more=(), scratch=(), work=LIGHT, alias=None):
        nonlocal last
        work = 10**6 * next(weights, 1)
        ins = [*first, last, *ins]
        res = call(kernel, name, ins, [VMEM] * len(ins), [*outs, (FLAG, F32), *more], scratch, work, alias or {})
        last = res[len(outs)]
        return [*res[: len(outs)], *res[len(outs) + 1 :]]

    step_outs = [((chunk, tokens, width), BF16), ((slots, rows, both), BF16)]
    slope_out = ((slots, chunk, tokens, width), F32)
    part_out = ((slots, rows, both), BF16)
    grad, proj, slope, part, next_slope, next_part, acts, top, mix_act, mix_grad, info = call(
        functools.partial(first_kernel, top_pair),
        "first",
        [
            pltpu.with_memory_space_constraint(x, pltpu.HBM)
            for x in (section_sizes, proj_blocks.transpose(1, 0, 2), grad_out, activations[0], mixing[0], proj_tiles[0])
        ],
        [HBM] * 6,
        [
            *step_outs,
            slope_out,
            part_out,
            slope_out,
            part_out,
            (activations.shape[1:], BF16),
            (grad_out.shape, BF16),
            ((slots, heads, head_size, head_size + both), BF16),
            ((slots, heads, head_size + both, head_size), BF16),
            (FLAG, F32),
        ],
        [
            pltpu.SMEM(section_sizes.shape, jnp.int32),
            pltpu.SMEM((slots, 1, proj_blocks.shape[2]), jnp.int32),
            pltpu.VMEM(proj_tiles.shape[1:], BF16),
            pltpu.SemaphoreType.DMA((6 * slots + 4,)),
        ],
    )
    last = info
    slopes = [slope, next_slope]
    swap = [(i, i ^ 1) for i in range(sections)]
    grads = [([], []) for _ in range(pairs)]
    projs = [([], []) for _ in range(pairs)]
    hops = [[] for _ in range(pairs)]
    core = [[] for _ in range(pairs)]

    def keep(p, odd, even, grad, proj):
        for parity, there in ((0, even), (1, odd)):
            if there:
                grads[p][parity].append(grad)
                projs[p][parity].append(proj)
        if odd:
            core[p].append(lax.ppermute(grad, "pipe", swap))
        if even and p + 1 < pairs:
            source = sections - 2 - 2 * p
            hop = [(source, source - 1)]
            if len(hops[p]) >= count - 2:
                hop = [(i, (i - 1) % sections) for i in range(sections)]
            hops[p].append(lax.ppermute(grad, "pipe", hop))

    def top_step(at):
        ins, scratch = [core[0][at - 1], slopes[at - 1]], []
        if at < count:
            ins += [top, acts, mix_act]
            scratch.append(pltpu.VMEM(slope_out[0], F32))
        kernel = functools.partial(top_kernel, top_pair, at, at < count)
        keep(0, at < count, True, *in_turn(kernel, "top", [info, mix_grad], ins, step_outs, scratch=scratch))

    def step(p, parity, at):
        source = hops[p - 1][at] if parity else core[p][at]
        kernel = functools.partial(step_kernel, top_pair - p, parity)
        keep(p, parity, not parity, *in_turn(kernel, "step", [info, mix_grad], [source, slopes[at]], step_outs))

    class Sum:
        def __init__(self, value, turns):
            self.mine, self.turns = value, turns
            self.go()

        def go(self):
            self.other = exchange(self.mine, *self.turns.pop(0))

        def turn(self, work=LIGHT):
            self.mine = in_turn(add_kernel, "add", [self.mine, self.other], [], [(self.mine.shape, BF16)], work=work)[0]
            self.go()

    def collect():
        ins = [grad for pair in grads for parity in (1, 0) for grad in pair[parity]]
        return in_turn(functools.partial(collect_kernel, pairs), "collect", [], ins, [(grad_out.shape, BF16)])[0]

    def sketch(group):
        out = ((slots, 2, rows, chunk * both), BF16)
        kernel = functools.partial(widen_kernel, group, chunk)
        wide = in_turn(kernel, "widen", [act_sum.mine, act_sum.other], [], [out])[0]
        ins = []
        for p in range(pairs):
            for parity in (1, 0):
                ins += projs[p][parity][2 * group : 2 * group + 2]
        kernel = functools.partial(sketch_kernel, pairs, scale)
        out = ((slots, 2 * chunk, rank // 2, both), BF16)
        return in_turn(kernel, "sketch", [info], [*ins, wide], [out])[0]

    low = pairs - 1
    act_turns = list(swaps(("tensor",)))
    turns = list(swaps(("dp", "tensor")))
    keep(0, True, False, grad, proj)
    slope, act_part = in_turn(
        functools.partial(beside_kernel, top_pair),
        "beside",
        [info, acts, mix_act],
        [part, next_part],
        [slope_out, ((2, *part_out[0]), BF16)],
        scratch=[pltpu.VMEM(*part_out)],
    )
    slopes.append(slope)
    act_sum = Sum(act_part, act_turns)
    top_step(1)
    top_step(2)
    kernel = functools.partial(slope_kernel, top_pair, 3 * chunk)
    slopes += in_turn(kernel, "slope", [info, acts, mix_act], [], [slope_out])
    while act_sum.turns:
        act_sum.turn()
    top_step(3)
    for p in range(1, pairs):
        step(p, 1, 0)
        if p == 1:
            top_step(count)
        else:
            step(p - 1, 0, 3)
        step(p, 1, 1)
        step(p, 0, 0)
        step(p, 0, 1)
        if p < low:
            step(p, 1, 2)
            step(p, 1, 3)
            step(p, 0, 2)
    early = Sum(sketch(0), list(swaps(("tensor", "dp"))))
    step(low, 1, 2)
    step(low, 1, 3)
    step(low, 0, 2)
    step(low, 0, 3)
    late = Sum(sketch(1), list(turns))
    segment_out = None
    while late.turns:
        if early.turns:
            early.turn()
        late.turn()
        if segment_out is None:
            segment_out = collect()
    done = ((slots, 2 * chunk, rank * rank), F32)
    (begun,) = in_turn(rows_kernel, "rows", [early.mine, early.other], [], [done])
    ins = [last, begun, late.mine, late.other]
    (total,) = call(last_kernel, "last", ins, [VMEM] * 4, [((slots, micro, rank * rank), F32)])

    return (segment_out[None], total[None])


def solution(mesh):
    return jax.shard_map(
        shards,
        mesh=mesh,
        in_specs=(
            P(None, "dp", "tensor"),
            P("pipe", None, None, "dp", "tensor"),
            P("pipe", None, "tensor", None, None),
            P("pipe", None, None, None, None),
            P("pipe", None, None),
            P(),
        ),
        out_specs=(P("pipe", None, "dp", "tensor"), P("pipe", None, None, None)),
        check_vma=False,
    )
```
